32 devices in a mesh: freq: 4 (over y, x), ga: 4 (over z), band: 2 (over core).
Axes of the slice: x: 2, y: 2, z: 4, core: 2. Of those that a mesh axis runs over, the one named last changes fastest.
Arguments:
- pair_matrix: bfloat16 [16, 768, 2048], P('band', 'freq', 'ga'), may hold values from -0.29882812 to 0.29882812
- screened: bfloat16 [8, 2048, 2048], P('freq', None, 'ga'), may hold values from -0.125 to 0.125
- imag_freq: float32 [8], P('freq'), may hold values from 0.1 to 20
- quad_weight: float32 [8], P('freq'), may hold values from 0.05 to 2
- band_energy: float32 [256], replicated, may hold values from -12 to 12
- band_index: int32 [768], P('freq'), may hold values from 0 to 255
Outputs:
- sigma: float32 [16, 256], P('band')
The draws below stay inside these ranges and needn't reach their ends.
All inputs are finite; a program needn't handle non-finite values.
Results may differ from the reference program's by a relative error of at most 0.0003.
Values may be sent and summed in bfloat16 or wider, within the bound.
No kernel may reach another device: no remote copies, remote signals or barrier semaphores. Data moves between devices by JAX's collectives and lax.ppermute only.
A program may use at most 128 MiB of HBM per device.

```python
import math
import jax
import jax.numpy as jnp
from jax import lax

G = 2048
NW = 256
NBANDS = 256
N = 16
MB = 768
NF = 8


def plant(array, rng, low, top_value):
    extent = array.shape
    spot = [jax.random.randint(jax.random.fold_in(rng, axis), (), 0, extent[axis]) for axis in range(len(extent))]
    array = array.at[tuple(spot)].set(low)
    longest = extent.index(max(extent))
    spot[longest] = (spot[longest] + 1) % extent[longest]
    return array.at[tuple(spot)].set(top_value)


def shard_levels(rng, extent, cuts, low, high):
    gain, own = 1.0, jax.random.fold_in(rng, 6)
    for axis_at, blocks in cuts:
        draws = jnp.exp(jax.random.uniform(jax.random.fold_in(own, axis_at), (blocks,), jnp.float32, low / len(cuts), high / len(cuts)))
        gain = gain * jnp.repeat(draws, extent[axis_at] // blocks).reshape([-1 if axis == axis_at else 1 for axis in range(len(extent))])
    return gain


def normal_values(stream_key, extent, deviation, bound, split=(), kind=jnp.bfloat16):
    result = deviation * jax.random.normal(stream_key, extent, jnp.float32)
    if split:
        result = result * shard_levels(stream_key, extent, split, -0.22, 0.18)
    return jnp.clip(result, -bound, bound).astype(kind)


def setup_inputs(seed: int = 0) -> dict:
    arg_keys = jax.random.split(jax.random.key(seed), 7)
    pair_matrix = normal_values(arg_keys[0], (N, MB, G), 0.05, 0.29882812, ((0, 2), (1, 4), (2, 4)))
    screened = normal_values(arg_keys[1], (NF, G, G), G ** -0.5, 0.125, ((0, 4), (2, 4)))
    imag_freq = jnp.clip(jnp.exp(math.log(20.0) - 5.2983174 * jax.random.uniform(arg_keys[2], (NF,), jnp.float32) ** shard_levels(arg_keys[2], (NF,), ((0, 4),), -0.2, 0.2)), 0.1, 20.0)
    quad_weight = jnp.clip(jnp.exp(math.log(2.0) - 3.6888794 * jax.random.uniform(arg_keys[3], (NF,), jnp.float32) ** shard_levels(arg_keys[3], (NF,), ((0, 4),), -0.2, 0.2)), 0.05, 2.0)
    band_energy = jnp.clip(jax.random.uniform(arg_keys[4], (NBANDS,), jnp.float32, -12.0, 12.0), -12.0, 12.0)
    band_index = plant(jax.random.randint(arg_keys[5], (MB,), 0, NBANDS), jax.random.fold_in(arg_keys[5], 1), 0, NBANDS - 1).astype(jnp.int32)
    return dict(pair_matrix=pair_matrix, screened=screened, imag_freq=imag_freq, quad_weight=quad_weight, band_energy=band_energy, band_index=band_index)


omega_low = -10.0
omega_span = 20.0


def make_grid(count):
    return omega_low + omega_span * jnp.arange(count, dtype=jnp.float32) / (count - 1)


def reference(pair_matrix, screened, imag_freq, quad_weight, band_energy, band_index):
    n_all, m_all, g_all = pair_matrix.shape
    rows = pair_matrix.reshape(n_all * m_all, g_all)
    rows_wide = rows.astype(jnp.float32)
    energies = band_energy[band_index.astype(jnp.int32)]
    omega_grid = make_grid(NW)
    offsets = omega_grid[None, :] - energies[:, None]

    def one_freq(inputs):
        w_mat, nu_val, weight_val = inputs
        product = jnp.dot(rows, w_mat, preferred_element_type=jnp.float32)
        contract = jnp.sum(product * rows_wide, axis=-1).reshape(n_all, m_all)
        kernel = offsets / (offsets * offsets + nu_val * nu_val)
        return (-weight_val / math.pi) * jnp.dot(contract, kernel, precision=lax.Precision.HIGHEST)

    partials = lax.map(one_freq, (screened, imag_freq, quad_weight))
    return jnp.sum(partials, axis=0)
```

```python
import functools
import math

import jax
import jax.numpy as jnp
from jax import lax
from jax.experimental import pallas as pl
from jax.experimental.pallas import tpu as pltpu
from jax.sharding import PartitionSpec as P

NW = 256

omega_low = -10.0
omega_span = 20.0


def make_grid(count):
    return omega_low + omega_span * jnp.arange(count, dtype=jnp.float32) / (count - 1)


def lookup(indices, table):
    hit = indices[:, None] == jnp.arange(table.shape[0], dtype=jnp.int32)[None, :]
    return jnp.sum(jnp.where(hit, table[None, :], 0.0), axis=1)


def from_behind(block, axis, distance):
    devices = range(lax.axis_size(axis))
    route = [((i - distance) % len(devices), i) for i in devices]
    return lax.ppermute(block, axis, route)


def flip(block, axis, bits):
    return lax.ppermute(block, axis, [(i, i ^ bits) for i in range(lax.axis_size(axis))])


def contribute(full_rows, panel_rows, w_mat, nu_val, weight_val, energies, omega_grid, n_dev):
    product = jnp.dot(full_rows, w_mat, preferred_element_type=jnp.float32)
    contract = jnp.sum(product * panel_rows.astype(jnp.float32), axis=-1).reshape(n_dev, -1)
    offsets = omega_grid[None, :] - energies[:, None]
    kernel = offsets / (offsets * offsets + nu_val * nu_val)
    return -weight_val / math.pi * jnp.dot(contract, kernel, precision=lax.Precision.HIGHEST)


def general(pair_matrix, screened, imag_freq, quad_weight, band_energy, band_index):
    n_dev, m_dev, g_panel = pair_matrix.shape
    f_dev = screened.shape[0]
    cycle_size = lax.axis_size("freq")
    cycle_pos = lax.axis_index("freq")
    full_pairs = lax.all_gather(pair_matrix, "ga", axis=2, tiled=True)
    g_all = full_pairs.shape[2]
    omega_grid = make_grid(NW)
    sigma_part = jnp.zeros((n_dev, NW), jnp.float32)
    panel_rows = pair_matrix.reshape(n_dev * m_dev, g_panel)
    full_rows = full_pairs.reshape(n_dev * m_dev, g_all)
    energies = lookup(band_index, band_energy)
    nu_all = lax.all_gather(imag_freq, "freq", axis=0, tiled=True)
    weight_all = lax.all_gather(quad_weight, "freq", axis=0, tiled=True)
    w_slab = screened
    for turn_index in range(cycle_size):
        source = jnp.mod(cycle_pos - turn_index, cycle_size)
        nu_vals = lax.dynamic_slice_in_dim(nu_all, source * f_dev, f_dev)
        weight_vals = lax.dynamic_slice_in_dim(weight_all, source * f_dev, f_dev)
        for slot in range(f_dev):
            sigma_part = sigma_part + contribute(
                full_rows, panel_rows, w_slab[slot], nu_vals[slot], weight_vals[slot],
                energies, omega_grid, n_dev,
            )
        if turn_index + 1 < cycle_size:
            w_slab = from_behind(w_slab, "freq", 1)
    return lax.psum(sigma_part, ("freq", "ga"))


def accumulate(contract, weight_ref, slot, out_ref, first, m_dev):
    for k in range(contract.shape[0] // m_dev):
        rows = contract[k * m_dev : (k + 1) * m_dev]
        term = rows * weight_ref[slot]
        out_ref[first + k] += jnp.sum(term.reshape(m_dev // 8, 8, NW), axis=0)


def near_kernel(n_slots, n_tile, m_dev, panel, where_ref, k_ref, own_ref, a_ref, b_ref, *rest):
    w_refs, (out_ref, left, own, w_all, k_all, sems, w_sems) = rest[:-7], rest[-7:]
    end, low = where_ref[0], where_ref[1]
    here = pl.multiple_of((1 - low) * panel, panel)
    there = pl.multiple_of(low * panel, panel)
    copies = [
        pltpu.make_async_copy(own_ref, own, sems.at[0]),
        pltpu.make_async_copy(own_ref, left.at[:, pl.ds(here, panel)], sems.at[1]),
    ]
    for c in copies:
        c.start()
    from_a = pltpu.make_async_copy(a_ref, left.at[:, pl.ds(there, panel)], sems.at[2])
    from_b = pltpu.make_async_copy(b_ref, left.at[:, pl.ds(there, panel)], sems.at[2])

    @pl.when(end == 1)
    def _():
        from_a.start()

    @pl.when(end == 0)
    def _():
        from_b.start()

    k_copy = pltpu.make_async_copy(k_ref, k_all, sems.at[3])
    k_copy.start()
    start_slots(where_ref, w_refs, w_all, w_sems, 2)
    out_ref[...] = jnp.zeros_like(out_ref)
    for c in copies:
        c.wait()
    from_a.wait()
    k_copy.wait()
    rows = n_tile * m_dev

    def one(slot, carry):
        pltpu.make_async_copy(w_all.at[slot], w_all.at[slot], w_sems.at[slot]).wait()
        for t in range(own.shape[0] // rows):
            at = slice(t * rows, (t + 1) * rows)
            y = jnp.dot(left[at], w_all[slot], preferred_element_type=jnp.float32)
            c = jnp.sum(y * own[at].astype(jnp.float32), axis=1, keepdims=True)
            accumulate(c, k_all, slot, out_ref, t * n_tile, m_dev)
        return carry

    lax.fori_loop(0, n_slots, one, 0)


def far_kernel(n_slots, n_tile, m_dev, panel, where_ref, k_ref, own_ref, a_ref, c_ref, d_ref, *rest):
    w_refs, (out_ref, own, far, other, left, w_all, k_all, sems, w_sems) = rest[:-9], rest[-9:]
    end = where_ref[0]
    copies = [
        pltpu.make_async_copy(own_ref, own, sems.at[0]),
        pltpu.make_async_copy(a_ref, other, sems.at[1]),
    ]
    for c in copies:
        c.start()
    far_c = pltpu.make_async_copy(c_ref, far, sems.at[2])
    far_d = pltpu.make_async_copy(d_ref, far, sems.at[2])
    left_own = pltpu.make_async_copy(own_ref, left, sems.at[3])
    left_far = pltpu.make_async_copy(d_ref, left, sems.at[3])

    @pl.when(end == 1)
    def _():
        far_c.start()
        left_own.start()

    @pl.when(end == 0)
    def _():
        far_d.start()
        left_far.start()

    k_copy = pltpu.make_async_copy(k_ref, k_all, sems.at[4])
    k_copy.start()
    start_slots(where_ref, w_refs, w_all, w_sems, 3)
    out_ref[...] = jnp.zeros_like(out_ref)
    for c in copies:
        c.wait()
    far_c.wait()
    left_own.wait()
    k_copy.wait()
    rows = n_tile * m_dev

    def one(slot, carry):
        pltpu.make_async_copy(w_all.at[slot], w_all.at[slot], w_sems.at[slot]).wait()
        for t in range(own.shape[0] // rows):
            at = slice(t * rows, (t + 1) * rows)
            y = jnp.dot(far[at], w_all[slot, :panel], preferred_element_type=jnp.float32)
            x = jnp.dot(left[at], w_all[slot, panel:], preferred_element_type=jnp.float32)
            z = y * own[at].astype(jnp.float32) + x * other[at].astype(jnp.float32)
            c = jnp.sum(z, axis=1, keepdims=True)
            accumulate(c, k_all, slot, out_ref, t * n_tile, m_dev)
        return carry

    lax.fori_loop(0, n_slots, one, 0)


def start_slots(where_ref, w_refs, w_all, w_sems, row_entry):
    slot, filled = 0, 0
    depth = w_all.shape[1]
    for ref in w_refs:
        if len(ref.shape) == 3:
            count = min(depth - filled, depth // 2 if row_entry == 3 else depth)
            begin = pl.multiple_of(where_ref[row_entry], 512)
            src = ref.at[where_ref[4], pl.ds(begin, count), :]
        else:
            count = ref.shape[0]
            src = ref
        dst = w_all.at[slot, filled : filled + count, :]
        pltpu.make_async_copy(src, dst, w_sems.at[slot]).start()
        filled += count
        if filled == depth:
            slot, filled = slot + 1, 0
    assert filled == 0


def run_kernel(body, where, k_part, mats, n_rows, slots, m_dev, n_lefts, left_width):
    panel = mats[0].shape[1]
    n_slots = k_part.shape[0]
    n_states = n_rows // m_dev
    n_tile = 2 if n_states % 2 == 0 else 1
    arrays = [w for slot in slots for w in slot]
    depth = 2 * panel
    scratch = [pltpu.VMEM((n_rows, left_width), jnp.bfloat16)]
    scratch += [pltpu.VMEM((n_rows, panel), jnp.bfloat16)] * (n_lefts - 1)
    scratch += [
        pltpu.VMEM((n_slots, depth, panel), jnp.bfloat16),
        pltpu.VMEM(k_part.shape, jnp.float32),
        pltpu.SemaphoreType.DMA((5,)),
        pltpu.SemaphoreType.DMA((n_slots,)),
    ]
    flops = 2 * n_rows * depth * panel * n_slots
    return pl.pallas_call(
        functools.partial(body, n_slots, n_tile, m_dev, panel),
        out_shape=jax.ShapeDtypeStruct((n_states, 8, NW), jnp.float32),
        in_specs=[pl.BlockSpec(memory_space=pltpu.SMEM)]
        + [pl.BlockSpec(memory_space=pl.ANY)] * (1 + len(mats) + len(arrays)),
        out_specs=pl.BlockSpec(memory_space=pltpu.VMEM),
        scratch_shapes=scratch,
        cost_estimate=pl.CostEstimate(flops=flops, bytes_accessed=n_slots * depth * panel * 2, transcendentals=0),
        compiler_params=pltpu.CompilerParams(vmem_limit_bytes=48 * 2**20),
    )(where, k_part, *mats, *arrays)


def square_line(pair_matrix, screened, imag_freq, quad_weight, band_energy, band_index):
    n_dev, m_dev, panel = pair_matrix.shape
    ga = lax.axis_index("ga")
    core = lax.axis_index("band")
    rows = n_dev * m_dev
    own = pair_matrix.reshape(rows, panel)
    end = (ga == 0) | (ga == 3)
    low = ga < 2
    near_at = jnp.where(ga == 0, 0, jnp.where(ga == 3, 2, 1)) * panel
    far_at = (ga + 2) % 4 * panel
    give_at = jnp.where(ga % 2 == 0, 3, 0) * panel
    where = jnp.stack([end, low, near_at, far_at, 1 - core]).astype(jnp.int32)

    outer = [(0, 1), (1, 0), (2, 3), (3, 2)]
    inner = [(1, 2), (2, 1)]
    outward = [(1, 0), (2, 3)]

    nodes = jnp.stack([imag_freq, quad_weight])
    node_sets = [nodes] + [flip(nodes, "freq", r) for r in (1, 2, 3)]

    def piece(start, count):
        return lax.dynamic_slice(screened, (core, start, 0), (1, count, panel))[0]

    given = lax.ppermute(piece(give_at, panel), "ga", outer)
    near_w = piece(near_at, 2 * panel)
    x1 = flip(near_w, "freq", 1)
    y1 = flip(near_w, "freq", 2)
    a_rows = lax.ppermute(own, "ga", outer)
    b_rows = lax.ppermute(own, "ga", inner)
    far_w = jnp.concatenate([piece(far_at, panel), given])
    x2 = flip(far_w, "freq", 1)
    y2 = flip(far_w, "freq", 2)
    d1a = flip(y1[:panel], "freq", 1)
    d1b = flip(x1[panel:], "freq", 2)
    d2a = flip(y2[:panel], "freq", 1)
    d2b = flip(x2[panel:], "freq", 2)
    given_o, x1_o, y1_o, x2_o, y2_o, d1a_o, d1b_o, d2a_o, d2b_o = (
        flip(w, "band", 1) for w in (given, x1, y1, x2, y2, d1a, d1b, d2a, d2b)
    )
    half = rows // 2
    cuts = [slice(0, half), slice(half, rows)]
    c_rows = [lax.ppermute(b_rows[cut], "ga", outward) for cut in cuts]
    d_rows = [lax.ppermute(a_rows[cut], "ga", inner) for cut in cuts]

    energies = lookup(band_index, band_energy)
    offsets = make_grid(NW)[None, :] - energies[:, None]
    ordered = [jnp.where(core == 0, s, s[:, ::-1]) for s in node_sets]
    nu = jnp.concatenate([s[0] for s in ordered])[:, None, None]
    weight = jnp.concatenate([s[1] for s in ordered])[:, None, None]
    k_all = (-weight / math.pi) * (offsets / (offsets * offsets + nu * nu))

    near = functools.partial(run_kernel, near_kernel, where, n_lefts=2, left_width=2 * panel, m_dev=m_dev, n_rows=rows, mats=(own, a_rows, b_rows))
    s1 = near(k_part=k_all[:6], slots=[[near_w], [screened], [x1], [x1_o], [y1], [y1_o]])
    s2 = near(k_part=k_all[6:], slots=[[d1a, d1b], [d1a_o, d1b_o]])
    first = [[far_w], [screened, given_o], [x2], [x2_o], [y2], [y2_o]]
    second = [[d2a, d2b], [d2a_o, d2b_o]]
    parts = []
    for i, cut in enumerate(cuts):
        mats = (own[cut], a_rows[cut], c_rows[i], d_rows[i])
        if i == 0:
            parts.append(
                run_kernel(far_kernel, where, k_all[:6], mats, half, first, m_dev, 4, panel)
                + run_kernel(far_kernel, where, k_all[6:], mats, half, second, m_dev, 4, panel)
            )
        else:
            parts.append(run_kernel(far_kernel, where, k_all, mats, half, first + second, m_dev, 4, panel))
    sigma = jnp.sum(s1 + s2 + jnp.concatenate(parts), axis=1)
    for axis in ("freq", "ga"):
        t1, t2, t3 = (flip(sigma, axis, r) for r in (1, 2, 3))
        sigma = (sigma + t1) + (t2 + t3)
    return sigma


def solution(mesh):
    placed = (P("band", "freq", "ga"), P("freq", None, "ga"), P("freq"), P("freq"), P(), P("freq"))
    fits = mesh.shape["freq"] == 4 and mesh.shape["ga"] == 4 and mesh.shape["band"] == 2
    return jax.shard_map(
        square_line if fits else general,
        mesh=mesh, in_specs=placed, out_specs=P("band", None), check_vma=False,
    )
```

```python
import functools
import math

import jax
import jax.numpy as jnp
from jax import lax
from jax.experimental import pallas as pl
from jax.experimental.pallas import tpu as pltpu
from jax.sharding import PartitionSpec as P

NW = 256

omega_low = -10.0
omega_span = 20.0


def make_grid(count):
    return omega_low + omega_span * jnp.arange(count, dtype=jnp.float32) / (count - 1)


def lookup(indices, table):
    hit = indices[:, None] == jnp.arange(table.shape[0], dtype=jnp.int32)[None, :]
    return jnp.sum(jnp.where(hit, table[None, :], 0.0), axis=1)


def from_behind(block, axis, distance):
    devices = range(lax.axis_size(axis))
    route = [((i - distance) % len(devices), i) for i in devices]
    return lax.ppermute(block, axis, route)


def flip(block, axis, bits):
    return lax.ppermute(block, axis, [(i, i ^ bits) for i in range(lax.axis_size(axis))])


def contribute(full_rows, panel_rows, w_mat, nu_val, weight_val, energies, omega_grid, n_dev):
    product = jnp.dot(full_rows, w_mat, preferred_element_type=jnp.float32)
    contract = jnp.sum(product * panel_rows.astype(jnp.float32), axis=-1).reshape(n_dev, -1)
    offsets = omega_grid[None, :] - energies[:, None]
    kernel = offsets / (offsets * offsets + nu_val * nu_val)
    return -weight_val / math.pi * jnp.dot(contract, kernel, precision=lax.Precision.HIGHEST)


def general(pair_matrix, screened, imag_freq, quad_weight, band_energy, band_index):
    n_dev, m_dev, g_panel = pair_matrix.shape
    f_dev = screened.shape[0]
    cycle_size = lax.axis_size("freq")
    cycle_pos = lax.axis_index("freq")
    full_pairs = lax.all_gather(pair_matrix, "ga", axis=2, tiled=True)
    g_all = full_pairs.shape[2]
    omega_grid = make_grid(NW)
    sigma_part = jnp.zeros((n_dev, NW), jnp.float32)
    panel_rows = pair_matrix.reshape(n_dev * m_dev, g_panel)
    full_rows = full_pairs.reshape(n_dev * m_dev, g_all)
    energies = lookup(band_index, band_energy)
    nu_all = lax.all_gather(imag_freq, "freq", axis=0, tiled=True)
    weight_all = lax.all_gather(quad_weight, "freq", axis=0, tiled=True)
    w_slab = screened
    for turn_index in range(cycle_size):
        source = jnp.mod(cycle_pos - turn_index, cycle_size)
        nu_vals = lax.dynamic_slice_in_dim(nu_all, source * f_dev, f_dev)
        weight_vals = lax.dynamic_slice_in_dim(weight_all, source * f_dev, f_dev)
        for slot in range(f_dev):
            sigma_part = sigma_part + contribute(
                full_rows, panel_rows, w_slab[slot], nu_vals[slot], weight_vals[slot],
                energies, omega_grid, n_dev,
            )
        if turn_index + 1 < cycle_size:
            w_slab = from_behind(w_slab, "freq", 1)
    return lax.psum(sigma_part, ("freq", "ga"))


def accumulate(contract, weight_ref, slot, out_ref, first, m_dev):
    for k in range(contract.shape[0] // m_dev):
        rows = contract[k * m_dev : (k + 1) * m_dev]
        term = rows * weight_ref[slot]
        out_ref[first + k] += jnp.sum(term.reshape(m_dev // 8, 8, NW), axis=0)


def choose(flag, yes, no):
    @pl.when(flag == 1)
    def _():
        yes.start()

    @pl.when(flag == 0)
    def _():
        no.start()


def near_kernel(tile, m_dev, where_ref, k_ref, own_ref, a_ref, b_ref, w_ref, out_ref, left, own, w_all, k_all, sems, w_sems):
    n_slots, depth, panel = w_all.shape
    end, low = where_ref[0], where_ref[1]
    here = left.at[:, pl.ds(pl.multiple_of((1 - low) * panel, panel), panel)]
    there = left.at[:, pl.ds(pl.multiple_of(low * panel, panel), panel)]
    waits = [
        pltpu.make_async_copy(own_ref, own, sems.at[0]),
        pltpu.make_async_copy(own_ref, here, sems.at[1]),
        pltpu.make_async_copy(k_ref, k_all, sems.at[3]),
    ]
    for c in waits:
        c.start()
    near = pltpu.make_async_copy(a_ref, there, sems.at[2])
    choose(end, near, pltpu.make_async_copy(b_ref, there, sems.at[2]))
    slots = [pltpu.make_async_copy(w_ref.at[s, :depth, :], w_all.at[s], w_sems.at[s]) for s in range(n_slots)]
    for c in slots:
        c.start()
    out_ref[...] = jnp.zeros_like(out_ref)
    for c in waits + [near]:
        c.wait()

    def one(slot, carry):
        pltpu.make_async_copy(w_all.at[slot], w_all.at[slot], w_sems.at[slot]).wait()
        for t in range(own.shape[0] // tile):
            at = slice(t * tile, (t + 1) * tile)
            y = jnp.dot(left[at], w_all[slot], preferred_element_type=jnp.float32)
            c = jnp.sum(y * own[at].astype(jnp.float32), axis=1, keepdims=True)
            accumulate(c, k_all, slot, out_ref, t * (tile // m_dev), m_dev)
        return carry

    lax.fori_loop(0, n_slots, one, 0)


def far_kernel(tile, m_dev, begin, where_ref, k_ref, own_ref, a_ref, c_ref, d_ref, w_ref, out_ref, own, far, other, left, w_all, k_all, sems, w_sems):
    n_slots, _, panel = w_all.shape
    end = where_ref[0]
    mine = own_ref.at[begin : begin + own.shape[0], :]
    theirs = a_ref.at[begin : begin + own.shape[0], :]
    waits = [
        pltpu.make_async_copy(mine, own, sems.at[0]),
        pltpu.make_async_copy(theirs, other, sems.at[1]),
        pltpu.make_async_copy(k_ref, k_all, sems.at[4]),
    ]
    for c in waits:
        c.start()
    far_copy = pltpu.make_async_copy(c_ref, far, sems.at[2])
    choose(end, far_copy, pltpu.make_async_copy(d_ref, far, sems.at[2]))
    left_copy = pltpu.make_async_copy(mine, left, sems.at[3])
    choose(end, left_copy, pltpu.make_async_copy(d_ref, left, sems.at[3]))
    slots = [pltpu.make_async_copy(w_ref.at[s], w_all.at[s], w_sems.at[s]) for s in range(n_slots)]
    for c in slots:
        c.start()
    out_ref[...] = jnp.zeros_like(out_ref)
    for c in waits + [far_copy, left_copy]:
        c.wait()

    def one(slot, carry):
        pltpu.make_async_copy(w_all.at[slot], w_all.at[slot], w_sems.at[slot]).wait()
        for t in range(own.shape[0] // tile):
            at = slice(t * tile, (t + 1) * tile)
            y = jnp.dot(far[at], w_all[slot, :panel], preferred_element_type=jnp.float32)
            z = y * own[at].astype(jnp.float32)
            x = jnp.dot(left[at], w_all[slot, panel:], preferred_element_type=jnp.float32)
            z = z + x * other[at].astype(jnp.float32)
            c = jnp.sum(z, axis=1, keepdims=True)
            accumulate(c, k_all, slot, out_ref, t * (tile // m_dev), m_dev)
        return carry

    lax.fori_loop(0, n_slots, one, 0)


def run_kernel(body, where, k_part, mats, w_set, n_rows, m_dev, n_lefts, wide):
    panel = mats[0].shape[1]
    n_slots, depth = k_part.shape[0], 2 * panel
    n_states = n_rows // m_dev
    scratch = [pltpu.VMEM((n_rows, panel * wide), jnp.bfloat16)]
    scratch += [pltpu.VMEM((n_rows, panel), jnp.bfloat16)] * (n_lefts - 1)
    scratch += [
        pltpu.VMEM((n_slots, depth, panel), jnp.bfloat16),
        pltpu.VMEM(k_part.shape, jnp.float32),
        pltpu.SemaphoreType.DMA((5,)),
        pltpu.SemaphoreType.DMA((n_slots,)),
    ]
    flops = 2 * n_rows * depth * panel * n_slots
    return pl.pallas_call(
        body,
        out_shape=jax.ShapeDtypeStruct((n_states, 8, NW), jnp.float32),
        in_specs=[pl.BlockSpec(memory_space=pltpu.SMEM)]
        + [pl.BlockSpec(memory_space=pl.ANY)] * (2 + len(mats)),
        out_specs=pl.BlockSpec(memory_space=pltpu.VMEM),
        scratch_shapes=scratch,
        cost_estimate=pl.CostEstimate(flops=flops, bytes_accessed=n_slots * depth * panel * 2, transcendentals=0),
        compiler_params=pltpu.CompilerParams(vmem_limit_bytes=48 * 2**20),
    )(where, k_part, *mats, w_set)


def split3(x):
    hi = lax.reduce_precision(x, 8, 7)
    mid = lax.reduce_precision(x - hi, 8, 7)
    return jnp.stack([hi, mid, (x - hi) - mid])


def square_line(pair_matrix, screened, imag_freq, quad_weight, band_energy, band_index):
    n_dev, m_dev, panel = pair_matrix.shape
    ga = lax.axis_index("ga")
    core = lax.axis_index("band")
    rows = n_dev * m_dev
    own = pair_matrix.reshape(rows, panel)
    end = (ga == 0) | (ga == 3)
    low = ga < 2
    near_at = jnp.where(ga == 0, 0, jnp.where(ga == 3, 2, 1)) * panel
    far_at = (ga + 2) % 4 * panel
    give_at = jnp.where(ga % 2 == 0, 3, 0) * panel
    where = jnp.stack([end, low]).astype(jnp.int32)

    outer = [(0, 1), (1, 0), (2, 3), (3, 2)]
    inner = [(1, 2), (2, 1)]
    outward = [(1, 0), (2, 3)]

    def piece(start, count):
        return lax.dynamic_slice(screened, (core, start, 0), (1, count, panel))[0]

    given = lax.ppermute(piece(give_at, panel), "ga", outer)
    node = split3(jnp.stack([imag_freq[core], quad_weight[core]])).reshape(1, 6)
    node = jnp.pad(node, ((0, 15), (0, panel - 6))).astype(jnp.bfloat16)
    near_w = jnp.concatenate([piece(near_at, 2 * panel), node])
    near_all = lax.all_gather(near_w, ("freq", "band"))
    a_rows = lax.ppermute(own, "ga", outer)
    b_rows = lax.ppermute(own, "ga", inner)
    far_w = jnp.concatenate([piece(far_at, panel), given])
    far_all = lax.all_gather(far_w, ("freq", "band"))
    half = rows // 2
    begins = (0, half)
    c_rows = [lax.ppermute(b_rows[i : i + half], "ga", outward) for i in begins]
    d_rows = [lax.ppermute(a_rows[i : i + half], "ga", inner) for i in begins]

    energies = lookup(band_index, band_energy)
    offsets = make_grid(NW)[None, :] - energies[:, None]
    nodes = near_all[:, 2 * panel, :6].astype(jnp.float32).reshape(-1, 3, 2)
    nodes = (nodes[:, 0] + nodes[:, 1]) + nodes[:, 2]
    nu, weight = nodes[:, 0, None, None], nodes[:, 1, None, None]
    k_all = (-weight / math.pi) * (offsets / (offsets * offsets + nu * nu))

    tile = 4 * m_dev
    near = run_kernel(
        functools.partial(near_kernel, tile, m_dev),
        where, k_all, (own, a_rows, b_rows), near_all, rows, m_dev, 2, 2,
    )
    parts = [
        run_kernel(
            functools.partial(far_kernel, tile, m_dev, i),
            where, k_all, (own, a_rows, c_rows[n], d_rows[n]), far_all, half, m_dev, 4, 1,
        )
        for n, i in enumerate(begins)
    ]
    sigma = jnp.sum(near + jnp.concatenate(parts), axis=1)
    for axis in ("freq", "ga"):
        t1, t2, t3 = (flip(sigma, axis, r) for r in (1, 2, 3))
        sigma = (sigma + t1) + (t2 + t3)
    return sigma


def on_device(pair_matrix, screened, *rest):
    sizes = tuple(lax.axis_size(a) for a in ("freq", "ga", "band"))
    fits = sizes == (4, 4, 2) and screened.shape[0] == 2 and pair_matrix.shape[0] % 8 == 0
    return (square_line if fits else general)(pair_matrix, screened, *rest)


def solution(mesh):
    placed = (P("band", "freq", "ga"), P("freq", None, "ga"), P("freq"), P("freq"), P(), P("freq"))
    return jax.shard_map(
        on_device, mesh=mesh, in_specs=placed, out_specs=P("band", None), check_vma=False
    )
```

```python
import functools
import math

import jax
import jax.numpy as jnp
from jax import lax
from jax.experimental import pallas as pl
from jax.experimental.pallas import tpu as pltpu
from jax.sharding import PartitionSpec as P

NW = 256

omega_low = -10.0
omega_span = 20.0


def make_grid(count):
    return omega_low + omega_span * jnp.arange(count, dtype=jnp.float32) / (count - 1)


def lookup(indices, table):
    hit = indices[:, None] == jnp.arange(table.shape[0], dtype=jnp.int32)[None, :]
    return jnp.sum(jnp.where(hit, table[None, :], 0.0), axis=1)


def from_behind(block, axis, distance):
    devices = range(lax.axis_size(axis))
    route = [((i - distance) % len(devices), i) for i in devices]
    return lax.ppermute(block, axis, route)


def flip(block, axis, bits):
    return lax.ppermute(block, axis, [(i, i ^ bits) for i in range(lax.axis_size(axis))])


def contribute(full_rows, panel_rows, w_mat, nu_val, weight_val, energies, omega_grid, n_dev):
    product = jnp.dot(full_rows, w_mat, preferred_element_type=jnp.float32)
    contract = jnp.sum(product * panel_rows.astype(jnp.float32), axis=-1).reshape(n_dev, -1)
    offsets = omega_grid[None, :] - energies[:, None]
    kernel = offsets / (offsets * offsets + nu_val * nu_val)
    return -weight_val / math.pi * jnp.dot(contract, kernel, precision=lax.Precision.HIGHEST)


def general(pair_matrix, screened, imag_freq, quad_weight, band_energy, band_index):
    n_dev, m_dev, g_panel = pair_matrix.shape
    f_dev = screened.shape[0]
    cycle_size = lax.axis_size("freq")
    cycle_pos = lax.axis_index("freq")
    full_pairs = lax.all_gather(pair_matrix, "ga", axis=2, tiled=True)
    g_all = full_pairs.shape[2]
    omega_grid = make_grid(NW)
    sigma_part = jnp.zeros((n_dev, NW), jnp.float32)
    panel_rows = pair_matrix.reshape(n_dev * m_dev, g_panel)
    full_rows = full_pairs.reshape(n_dev * m_dev, g_all)
    energies = lookup(band_index, band_energy)
    nu_all = lax.all_gather(imag_freq, "freq", axis=0, tiled=True)
    weight_all = lax.all_gather(quad_weight, "freq", axis=0, tiled=True)
    w_slab = screened
    for turn_index in range(cycle_size):
        source = jnp.mod(cycle_pos - turn_index, cycle_size)
        nu_vals = lax.dynamic_slice_in_dim(nu_all, source * f_dev, f_dev)
        weight_vals = lax.dynamic_slice_in_dim(weight_all, source * f_dev, f_dev)
        for slot in range(f_dev):
            sigma_part = sigma_part + contribute(
                full_rows, panel_rows, w_slab[slot], nu_vals[slot], weight_vals[slot],
                energies, omega_grid, n_dev,
            )
        if turn_index + 1 < cycle_size:
            w_slab = from_behind(w_slab, "freq", 1)
    return lax.psum(sigma_part, ("freq", "ga"))


def choose(flag, yes, no):
    @pl.when(flag == 1)
    def _():
        yes.start()

    @pl.when(flag == 0)
    def _():
        no.start()


def reduce_rows(y_ref, right_ref, weight_ref, slot, out_ref, first, m_dev):
    for k in range(y_ref.shape[0] // m_dev):
        at = slice(k * m_dev, (k + 1) * m_dev)
        z = y_ref[at] * right_ref[at].astype(jnp.float32)
        term = jnp.sum(z, axis=1, keepdims=True) * weight_ref[slot]
        out_ref[first + k] += jnp.sum(term.reshape(m_dev // 8, 8, NW), axis=0)


def alternate(n_slots, w_all, w_sems, y0, y1, dot0, dot1, sum0, sum1):
    y1[...] = jnp.zeros_like(y1)

    def one(slot, carry):
        pltpu.make_async_copy(w_all.at[slot], w_all.at[slot], w_sems.at[slot]).wait()
        y0[...] = dot0(slot)
        sum1(y1, jnp.maximum(slot - 1, 0))
        y1[...] = dot1(slot)
        sum0(y0, slot)
        return carry

    lax.fori_loop(0, n_slots, one, 0)
    sum1(y1, n_slots - 1)


def start_slots(where_ref, plan, refs, w_all, w_sems, panel):
    for slot, pieces in enumerate(plan):
        at = 0
        for index, lead, begin, count in pieces:
            if lead is None:
                src = refs[index].at[begin : begin + count, :]
            else:
                src = refs[index].at[where_ref[lead], pl.ds(pl.multiple_of(where_ref[begin], panel), count), :]
            pltpu.make_async_copy(src, w_all.at[slot, at : at + count, :], w_sems.at[slot]).start()
            at += count


def near_kernel(plan, m_dev, where_ref, k_ref, own_ref, a_ref, b_ref, *rest):
    w_refs, (out_ref, left, own, w_all, k_all, y0, y1, sems, w_sems) = rest[:-9], rest[-9:]
    n_slots, depth, panel = w_all.shape
    end, low = where_ref[0], where_ref[1]
    here = left.at[:, pl.ds(pl.multiple_of((1 - low) * panel, panel), panel)]
    there = left.at[:, pl.ds(pl.multiple_of(low * panel, panel), panel)]
    waits = [
        pltpu.make_async_copy(own_ref, own, sems.at[0]),
        pltpu.make_async_copy(own_ref, here, sems.at[1]),
        pltpu.make_async_copy(k_ref, k_all, sems.at[3]),
    ]
    for c in waits:
        c.start()
    near = pltpu.make_async_copy(a_ref, there, sems.at[2])
    choose(end, near, pltpu.make_async_copy(b_ref, there, sems.at[2]))
    start_slots(where_ref, plan, w_refs, w_all, w_sems, panel)
    out_ref[...] = jnp.zeros_like(out_ref)
    for c in waits + [near]:
        c.wait()
    tile = y0.shape[0]
    states = tile // m_dev

    def product(t):
        return lambda s: jnp.dot(left[t * tile : (t + 1) * tile], w_all[s], preferred_element_type=jnp.float32)

    def total(t):
        right = own.at[t * tile : (t + 1) * tile, :]
        return lambda y, s: reduce_rows(y, right, k_all, s, out_ref, t * states, m_dev)

    alternate(n_slots, w_all, w_sems, y0, y1, product(0), product(1), total(0), total(1))


def far_kernel(plan, m_dev, begin, where_ref, k_ref, own_ref, a_ref, c_ref, d_ref, *rest):
    w_refs, (out_ref, far, own, other, left, w_all, k_all, y0, y1, sems, w_sems) = rest[:-11], rest[-11:]
    n_slots, _, panel = w_all.shape
    end = where_ref[0]
    mine = own_ref.at[begin : begin + own.shape[0], :]
    theirs = a_ref.at[begin : begin + own.shape[0], :]
    waits = [
        pltpu.make_async_copy(mine, own, sems.at[0]),
        pltpu.make_async_copy(theirs, other, sems.at[1]),
        pltpu.make_async_copy(k_ref, k_all, sems.at[4]),
    ]
    for c in waits:
        c.start()
    far_copy = pltpu.make_async_copy(c_ref, far, sems.at[2])
    choose(end, far_copy, pltpu.make_async_copy(d_ref, far, sems.at[2]))
    left_copy = pltpu.make_async_copy(mine, left, sems.at[3])
    choose(end, left_copy, pltpu.make_async_copy(d_ref, left, sems.at[3]))
    start_slots(where_ref, plan, w_refs, w_all, w_sems, panel)
    out_ref[...] = jnp.zeros_like(out_ref)
    for c in waits + [far_copy, left_copy]:
        c.wait()
    alternate(
        n_slots, w_all, w_sems, y0, y1,
        lambda s: jnp.dot(far[...], w_all[s, :panel], preferred_element_type=jnp.float32),
        lambda s: jnp.dot(left[...], w_all[s, panel:], preferred_element_type=jnp.float32),
        lambda y, s: reduce_rows(y, own, k_all, s, out_ref, 0, m_dev),
        lambda y, s: reduce_rows(y, other, k_all, s, out_ref, 0, m_dev),
    )


def run_kernel(body, where, k_part, mats, arrays, lefts, tile, n_rows, m_dev):
    panel = mats[0].shape[1]
    n_slots, depth = k_part.shape[0], 2 * panel
    scratch = [pltpu.VMEM((n_rows, width), jnp.bfloat16) for width in lefts]
    scratch += [
        pltpu.VMEM((n_slots, depth, panel), jnp.bfloat16),
        pltpu.VMEM(k_part.shape, jnp.float32),
        pltpu.VMEM((tile, panel), jnp.float32),
        pltpu.VMEM((tile, panel), jnp.float32),
        pltpu.SemaphoreType.DMA((5,)),
        pltpu.SemaphoreType.DMA((n_slots,)),
    ]
    flops = 2 * n_rows * depth * panel * n_slots
    return pl.pallas_call(
        body,
        out_shape=jax.ShapeDtypeStruct((n_rows // m_dev, 8, NW), jnp.float32),
        in_specs=[pl.BlockSpec(memory_space=pltpu.SMEM)]
        + [pl.BlockSpec(memory_space=pl.ANY)] * (1 + len(mats) + len(arrays)),
        out_specs=pl.BlockSpec(memory_space=pltpu.VMEM),
        scratch_shapes=scratch,
        cost_estimate=pl.CostEstimate(flops=flops, bytes_accessed=depth * panel, transcendentals=0),
        compiler_params=pltpu.CompilerParams(vmem_limit_bytes=48 * 2**20),
    )(where, k_part, *mats, *arrays)


def split3(x):
    hi = lax.reduce_precision(x, 8, 7)
    mid = lax.reduce_precision(x - hi, 8, 7)
    return jnp.stack([hi, mid, (x - hi) - mid])


def after(value, *others):
    return lax.optimization_barrier((value,) + others)[0]


def square_line(pair_matrix, screened, imag_freq, quad_weight, band_energy, band_index):
    n_dev, m_dev, panel = pair_matrix.shape
    ga = lax.axis_index("ga")
    core = lax.axis_index("band")
    rows = n_dev * m_dev
    own = pair_matrix.reshape(rows, panel)
    end = (ga == 0) | (ga == 3)
    low = ga < 2
    near_at = jnp.where(ga == 0, 0, jnp.where(ga == 3, 2, 1)) * panel
    far_at = (ga + 2) % 4 * panel
    give_at = jnp.where(ga % 2 == 0, 3, 0) * panel
    where = jnp.stack([end, low, near_at, far_at, core, 1 - core]).astype(jnp.int32)

    outer = [(0, 1), (1, 0), (2, 3), (3, 2)]
    inner = [(1, 2), (2, 1)]
    outward = [(1, 0), (2, 3)]

    def piece(start, count):
        return lax.dynamic_slice(screened, (core, start, 0), (1, count, panel))[0]

    def share(block):
        return flip(block, "band", 1)

    node = split3(jnp.stack([imag_freq[core], quad_weight[core]])).reshape(1, 6)
    node = jnp.pad(node, ((0, 15), (0, panel - 6))).astype(jnp.bfloat16)
    near_w = jnp.concatenate([piece(near_at, 2 * panel), node])

    given = lax.ppermute(piece(give_at, panel), "ga", outer)
    x1 = flip(near_w, "freq", 1)
    y1 = flip(near_w, "freq", 2)
    a_rows = lax.ppermute(after(own, given), "ga", outer)
    b_rows = lax.ppermute(own, "ga", inner)
    far_w = jnp.concatenate([piece(far_at, panel), given])
    d1a = flip(y1[:panel], "freq", 1)
    d1b = flip(x1[panel:], "freq", 2)
    x2 = flip(after(far_w, x1, y1), "freq", 1)
    x1_o, y1_o = share(after(x1, b_rows)), share(after(y1, a_rows))
    given_o = share(given)
    y2 = flip(after(far_w, d1a, d1b), "freq", 2)
    energies = lookup(band_index, band_energy)
    offsets = make_grid(NW)[None, :] - energies[:, None]
    mine = jnp.stack([imag_freq, quad_weight], axis=1)
    mine = jnp.where(core == 0, mine, mine[::-1])

    def weigh(nodes):
        nu, weight = nodes[:, 0, None, None], nodes[:, 1, None, None]
        return (-weight / math.pi) * (offsets / (offsets * offsets + nu * nu))

    def carried(*places):
        terms = jnp.stack([w[row, :6] for w, row in places]).astype(jnp.float32).reshape(-1, 3, 2)
        return (terms[:, 0] + terms[:, 1]) + terms[:, 2]

    k_here = weigh(jnp.concatenate([mine, carried((x1, 2 * panel), (y1, 2 * panel))]))

    whole, one = 2 * panel, panel

    def close(plan, k_part, arrays):
        return run_kernel(
            functools.partial(near_kernel, plan, m_dev), where, k_part,
            (own, a_rows, b_rows), arrays, (whole, one), rows // 2, rows, m_dev,
        )

    near_plan = [[(0, 4 + s, 2, whole)] for s in range(2)]
    near_plan += [[(r, None, 0, whole)] for r in (1, 2)]
    near = close(near_plan, k_here, (screened, x1, y1))
    d1a_o, d1b_o = share(after(d1a, near)), share(after(d1b, near))
    k_there = weigh(carried((x1_o, 2 * panel), (y1_o, 2 * panel), (d1b, panel), (d1b_o, panel)))

    corner_plan = [[(r, None, 0, whole)] for r in (0, 1)]
    corner_plan += [[(r, None, 0, one), (r + 1, None, 0, one)] for r in (2, 4)]
    corner = close(corner_plan, k_there, (x1_o, y1_o, d1a, d1b, d1a_o, d1b_o))
    d2a = flip(y2[:panel], "freq", 1)
    d2b = flip(x2[panel:], "freq", 2)
    x2_o, y2_o, d2a_o, d2b_o = (share(w) for w in (x2, y2, d2a, d2b))
    cuts = ((0, rows // 2), (rows // 2, rows // 4), (3 * rows // 4, rows // 4))
    c_rows, d_rows = [], []
    for n, (i, count) in enumerate(cuts):
        c_gate = ((), (near, *d_rows[:1]), (corner, *d_rows[1:]))[n]
        d_gate = ((), (near, *c_rows[:1]), (corner, *c_rows[1:]))[n]
        c_rows.append(lax.ppermute(after(b_rows[i : i + count], *c_gate), "ga", outward))
        d_rows.append(lax.ppermute(after(a_rows[i : i + count], *d_gate), "ga", inner))
    first = [[(0, 4 + s, 3, one), (1 + s, None, 0, one)] for s in range(2)]
    first += [[(r, None, 0, whole)] for r in (3, 4)]
    first_arrays = (screened, given, given_o, x2, y2)
    last_arrays = (x2_o, y2_o, d2a, d2b, d2a_o, d2b_o)

    def last(r):
        plan = [[(r + s, None, 0, whole)] for s in range(2)]
        return plan + [[(r + s, None, 0, one), (r + s + 1, None, 0, one)] for s in (2, 4)]

    def far(n, plan, k_part, arrays):
        i, count = cuts[n]
        return run_kernel(
            functools.partial(far_kernel, plan, m_dev, i), where, k_part,
            (own, a_rows, c_rows[n], d_rows[n]), arrays, (one,) * 4, count, count, m_dev,
        )

    parts = [far(0, first, k_here, first_arrays) + far(0, last(0), k_there, last_arrays)]
    k_all = jnp.concatenate([k_here, k_there])
    for n in (1, 2):
        parts.append(far(n, first + last(5), k_all, first_arrays + last_arrays))
    sigma = jnp.sum(near + corner + jnp.concatenate(parts), axis=1)
    for axis, bits in (("freq", 1), ("freq", 2), ("ga", 1), ("ga", 2)):
        sigma = sigma + flip(sigma, axis, bits)
    return sigma


def on_device(pair_matrix, screened, *rest):
    sizes = tuple(lax.axis_size(a) for a in ("freq", "ga", "band"))
    fits = sizes == (4, 4, 2) and screened.shape[0] == 2 and pair_matrix.shape[0] % 8 == 0
    return (square_line if fits else general)(pair_matrix, screened, *rest)


def solution(mesh):
    placed = (P("band", "freq", "ga"), P("freq", None, "ga"), P("freq"), P("freq"), P(), P("freq"))
    return jax.shard_map(
        on_device, mesh=mesh, in_specs=placed, out_specs=P("band", None), check_vma=False
    )
```

```python
import functools
import math

import jax
import jax.numpy as jnp
from jax import lax
from jax.experimental import pallas as pl
from jax.experimental.pallas import tpu as pltpu
from jax.sharding import PartitionSpec as P

NW = 256

omega_low = -10.0
omega_span = 20.0


def make_grid(count):
    return omega_low + omega_span * jnp.arange(count, dtype=jnp.float32) / (count - 1)


def lookup(indices, table):
    hit = indices[:, None] == jnp.arange(table.shape[0], dtype=jnp.int32)[None, :]
    return jnp.sum(jnp.where(hit, table[None, :], 0.0), axis=1)


def from_behind(block, axis, distance):
    devices = range(lax.axis_size(axis))
    route = [((i - distance) % len(devices), i) for i in devices]
    return lax.ppermute(block, axis, route)


def flip(block, axis, bits):
    return lax.ppermute(block, axis, [(i, i ^ bits) for i in range(lax.axis_size(axis))])


def contribute(full_rows, panel_rows, w_mat, nu_val, weight_val, energies, omega_grid, n_dev):
    product = jnp.dot(full_rows, w_mat, preferred_element_type=jnp.float32)
    contract = jnp.sum(product * panel_rows.astype(jnp.float32), axis=-1).reshape(n_dev, -1)
    offsets = omega_grid[None, :] - energies[:, None]
    kernel = offsets / (offsets * offsets + nu_val * nu_val)
    return -weight_val / math.pi * jnp.dot(contract, kernel, precision=lax.Precision.HIGHEST)


def general(pair_matrix, screened, imag_freq, quad_weight, band_energy, band_index):
    n_dev, m_dev, g_panel = pair_matrix.shape
    f_dev = screened.shape[0]
    cycle_size = lax.axis_size("freq")
    cycle_pos = lax.axis_index("freq")
    full_pairs = lax.all_gather(pair_matrix, "ga", axis=2, tiled=True)
    g_all = full_pairs.shape[2]
    omega_grid = make_grid(NW)
    sigma_part = jnp.zeros((n_dev, NW), jnp.float32)
    panel_rows = pair_matrix.reshape(n_dev * m_dev, g_panel)
    full_rows = full_pairs.reshape(n_dev * m_dev, g_all)
    energies = lookup(band_index, band_energy)
    nu_all = lax.all_gather(imag_freq, "freq", axis=0, tiled=True)
    weight_all = lax.all_gather(quad_weight, "freq", axis=0, tiled=True)
    w_slab = screened
    for turn_index in range(cycle_size):
        source = jnp.mod(cycle_pos - turn_index, cycle_size)
        nu_vals = lax.dynamic_slice_in_dim(nu_all, source * f_dev, f_dev)
        weight_vals = lax.dynamic_slice_in_dim(weight_all, source * f_dev, f_dev)
        for slot in range(f_dev):
            sigma_part = sigma_part + contribute(
                full_rows, panel_rows, w_slab[slot], nu_vals[slot], weight_vals[slot],
                energies, omega_grid, n_dev,
            )
        if turn_index + 1 < cycle_size:
            w_slab = from_behind(w_slab, "freq", 1)
    return lax.psum(sigma_part, ("freq", "ga"))


def choose(flag, yes, no):
    @pl.when(flag == 1)
    def _():
        yes.start()

    @pl.when(flag == 0)
    def _():
        no.start()


def reduce_rows(y_ref, right_ref, weight_ref, slot, out_ref, first, m_dev):
    for k in range(y_ref.shape[0] // m_dev):
        at = slice(k * m_dev, (k + 1) * m_dev)
        z = y_ref[at] * right_ref[at].astype(jnp.float32)
        term = jnp.sum(z, axis=1, keepdims=True) * weight_ref[slot]
        out_ref[first + k] += jnp.sum(term.reshape(m_dev // 8, 8, NW), axis=0)


def alternate(fetch, n_slots, y0, y1, dot0, dot1, sum0, sum1):
    y1[...] = jnp.zeros_like(y1)

    def one(slot, carry):
        fetch(slot + 2)
        fetch.wait(slot)
        y0[...] = dot0(slot)
        sum1(y1, jnp.maximum(slot - 1, 0))
        y1[...] = dot1(slot)
        sum0(y0, slot)
        return carry

    lax.fori_loop(0, n_slots, one, 0)
    sum1(y1, n_slots - 1)


class Fetch:
    def __init__(self, parts, w_all, sems):
        self.parts, self.w_all, self.sems = parts, w_all, sems

    def __call__(self, slot):
        last = self.w_all.shape[0] - 1
        safe = jnp.minimum(slot, last)
        at = 0
        for refs, count in self.parts:
            each = (last + 1) // len(refs)
            for n, ref in enumerate(refs):

                @pl.when((slot >= n * each) & (slot < (n + 1) * each))
                def _():
                    src = ref.at[jnp.clip(slot - n * each, 0, each - 1), :count, :]
                    pltpu.make_async_copy(src, self.w_all.at[safe, at : at + count, :], self.sems.at[safe]).start()

            at += count

    def wait(self, slot):
        pltpu.make_async_copy(self.w_all.at[slot], self.w_all.at[slot], self.sems.at[slot]).wait()


def near_kernel(m_dev, where_ref, k_ref, own_ref, a_ref, b_ref, w_ref, out_ref, left, own, w_all, k_all, y0, y1, sems, w_sems):
    n_slots, depth, panel = w_all.shape
    end, low = where_ref[0], where_ref[1]
    here = left.at[:, pl.ds(pl.multiple_of((1 - low) * panel, panel), panel)]
    there = left.at[:, pl.ds(pl.multiple_of(low * panel, panel), panel)]
    fetch = Fetch([((w_ref,), depth)], w_all, w_sems)
    fetch(0)
    mine = pltpu.make_async_copy(own_ref, here, sems.at[1])
    mine.start()
    near = pltpu.make_async_copy(a_ref, there, sems.at[2])
    choose(end, near, pltpu.make_async_copy(b_ref, there, sems.at[2]))
    late = [
        pltpu.make_async_copy(own_ref, own, sems.at[0]),
        pltpu.make_async_copy(k_ref, k_all, sems.at[3]),
    ]
    for c in late:
        c.start()
    fetch(1)
    out_ref[...] = jnp.zeros_like(out_ref)
    for c in [mine, near] + late:
        c.wait()
    tile = y0.shape[0]
    states = tile // m_dev

    def product(t):
        return lambda s: jnp.dot(left[t * tile : (t + 1) * tile], w_all[s], preferred_element_type=jnp.float32)

    def total(t):
        right = own.at[t * tile : (t + 1) * tile, :]
        return lambda y, s: reduce_rows(y, right, k_all, s, out_ref, t * states, m_dev)

    alternate(fetch, n_slots, y0, y1, product(0), product(1), total(0), total(1))


def far_kernel(m_dev, begin, where_ref, k_ref, own_ref, a_ref, c_ref, d_ref, f_ref, f_other_ref, x_ref, x_other_ref, out_ref, far, own, other, left, w_all, k_all, y0, y1, sems, w_sems):
    n_slots, _, panel = w_all.shape
    end = where_ref[0]
    mine = own_ref.at[begin : begin + own.shape[0], :]
    theirs = a_ref.at[begin : begin + own.shape[0], :]
    fetch = Fetch([((f_ref, f_other_ref), panel), ((x_ref, x_other_ref), panel)], w_all, w_sems)
    fetch(0)
    far_copy = pltpu.make_async_copy(c_ref, far, sems.at[2])
    choose(end, far_copy, pltpu.make_async_copy(d_ref, far, sems.at[2]))
    left_copy = pltpu.make_async_copy(mine, left, sems.at[3])
    choose(end, left_copy, pltpu.make_async_copy(d_ref, left, sems.at[3]))
    late = [
        pltpu.make_async_copy(mine, own, sems.at[0]),
        pltpu.make_async_copy(theirs, other, sems.at[1]),
        pltpu.make_async_copy(k_ref, k_all, sems.at[4]),
    ]
    for c in late:
        c.start()
    fetch(1)
    out_ref[...] = jnp.zeros_like(out_ref)
    for c in [far_copy, left_copy] + late:
        c.wait()
    alternate(
        fetch, n_slots, y0, y1,
        lambda s: jnp.dot(far[...], w_all[s, :panel], preferred_element_type=jnp.float32),
        lambda s: jnp.dot(left[...], w_all[s, panel:], preferred_element_type=jnp.float32),
        lambda y, s: reduce_rows(y, own, k_all, s, out_ref, 0, m_dev),
        lambda y, s: reduce_rows(y, other, k_all, s, out_ref, 0, m_dev),
    )


def run_kernel(body, where, k_part, mats, arrays, lefts, tile, n_rows, m_dev):
    panel = mats[0].shape[1]
    n_slots, depth = k_part.shape[0], 2 * panel
    scratch = [pltpu.VMEM((n_rows, width), jnp.bfloat16) for width in lefts]
    scratch += [
        pltpu.VMEM((n_slots, depth, panel), jnp.bfloat16),
        pltpu.VMEM(k_part.shape, jnp.float32),
        pltpu.VMEM((tile, panel), jnp.float32),
        pltpu.VMEM((tile, panel), jnp.float32),
        pltpu.SemaphoreType.DMA((5,)),
        pltpu.SemaphoreType.DMA((n_slots,)),
    ]
    flops = 2 * n_rows * depth * panel * n_slots
    return pl.pallas_call(
        body,
        out_shape=jax.ShapeDtypeStruct((n_rows // m_dev, 8, NW), jnp.float32),
        in_specs=[pl.BlockSpec(memory_space=pltpu.SMEM)]
        + [pl.BlockSpec(memory_space=pl.ANY)] * (1 + len(mats) + len(arrays)),
        out_specs=pl.BlockSpec(memory_space=pltpu.VMEM),
        scratch_shapes=scratch,
        cost_estimate=pl.CostEstimate(flops=flops, bytes_accessed=depth * panel, transcendentals=0),
        compiler_params=pltpu.CompilerParams(vmem_limit_bytes=48 * 2**20),
    )(where, k_part, *mats, *arrays)


def split3(x):
    hi = lax.reduce_precision(x, 8, 7)
    mid = lax.reduce_precision(x - hi, 8, 7)
    return jnp.stack([hi, mid, (x - hi) - mid])


def after(value, *others):
    return lax.optimization_barrier((value,) + others)[0]


def square_line(pair_matrix, screened, imag_freq, quad_weight, band_energy, band_index):
    n_dev, m_dev, panel = pair_matrix.shape
    ga = lax.axis_index("ga")
    core = lax.axis_index("band")
    rows = n_dev * m_dev
    own = pair_matrix.reshape(rows, panel)
    end = (ga == 0) | (ga == 3)
    low = ga < 2
    near_at = jnp.where(ga == 0, 0, jnp.where(ga == 3, 2, 1)) * panel
    far_at = (ga + 2) % 4 * panel
    give_at = jnp.where(ga % 2 == 0, 3, 0) * panel
    where = jnp.stack([end, low]).astype(jnp.int32)

    outer = [(0, 1), (1, 0), (2, 3), (3, 2)]
    inner = [(1, 2), (2, 1)]
    outward = [(1, 0), (2, 3)]

    def piece(start, count):
        return lax.dynamic_slice(screened, (core, start, 0), (1, count, panel))[0]

    node = split3(jnp.stack([imag_freq[core], quad_weight[core]])).reshape(1, 6)
    node = jnp.pad(node, ((0, 15), (0, panel - 6))).astype(jnp.bfloat16)
    near_w = jnp.concatenate([piece(near_at, 2 * panel), node])
    near_w = lax.all_gather(near_w, "freq")
    a_rows = lax.ppermute(own, "ga", outer)
    b_rows = lax.ppermute(own, "ga", inner)
    given = lax.ppermute(piece(give_at, panel), "ga", outer)
    near_o = flip(after(near_w, a_rows, b_rows, given), "band", 1)

    energies = lookup(band_index, band_energy)
    offsets = make_grid(NW)[None, :] - energies[:, None]

    def weigh(slots):
        nodes = slots[:, 2 * panel, :6].astype(jnp.float32).reshape(-1, 3, 2)
        nodes = (nodes[:, 0] + nodes[:, 1]) + nodes[:, 2]
        nu, weight = nodes[:, 0, None, None], nodes[:, 1, None, None]
        return (-weight / math.pi) * (offsets / (offsets * offsets + nu * nu))

    def close(slots, k_part):
        return run_kernel(
            functools.partial(near_kernel, m_dev), where, k_part,
            (own, a_rows, b_rows), (slots,), (2 * panel, panel), rows // 2, rows, m_dev,
        )

    k_here, k_there = weigh(near_w), weigh(near_o)
    near = close(near_w, k_here)
    near_other = close(near_o, k_there)

    far_w = lax.all_gather(after(piece(far_at, panel), a_rows, b_rows, given), "freq")
    cuts = ((0, rows // 2), (rows // 2, rows // 2))
    c_rows = [lax.ppermute(b_rows[i : i + count], "ga", outward) for i, count in cuts]
    d_rows = [lax.ppermute(a_rows[i : i + count], "ga", inner) for i, count in cuts]
    given_w = lax.all_gather(after(given, near, c_rows[0], d_rows[0]), "freq")
    far_o = flip(after(far_w, near_other, c_rows[0], d_rows[0]), "band", 1)
    given_o = flip(after(given_w, c_rows[1], d_rows[1]), "band", 1)
    k_all = jnp.concatenate([k_here, k_there])
    parts = [
        run_kernel(
            functools.partial(far_kernel, m_dev, i), where, k_all,
            (own, a_rows, c_rows[n], d_rows[n]), (far_w, far_o, given_w, given_o),
            (panel,) * 4, count, count, m_dev,
        )
        for n, (i, count) in enumerate(cuts)
    ]
    sigma = jnp.sum(near + near_other + jnp.concatenate(parts), axis=1)
    for axis in ("freq", "ga"):
        t1, t2, t3 = (flip(sigma, axis, r) for r in (1, 2, 3))
        sigma = (sigma + t1) + (t2 + t3)
    return sigma


def on_device(pair_matrix, screened, *rest):
    sizes = tuple(lax.axis_size(a) for a in ("freq", "ga", "band"))
    fits = sizes == (4, 4, 2) and screened.shape[0] == 2 and pair_matrix.shape[0] % 8 == 0
    return (square_line if fits else general)(pair_matrix, screened, *rest)


def solution(mesh):
    placed = (P("band", "freq", "ga"), P("freq", None, "ga"), P("freq"), P("freq"), P(), P("freq"))
    return jax.shard_map(
        on_device, mesh=mesh, in_specs=placed, out_specs=P("band", None), check_vma=False
    )
```

```python
import functools
import math

import jax
import jax.numpy as jnp
from jax import lax
from jax.experimental import pallas as pl
from jax.experimental.pallas import tpu as pltpu
from jax.sharding import PartitionSpec as P

NW = 256

omega_low = -10.0
omega_span = 20.0


def make_grid(count):
    return omega_low + omega_span * jnp.arange(count, dtype=jnp.float32) / (count - 1)


def lookup(indices, table):
    hit = indices[:, None] == jnp.arange(table.shape[0], dtype=jnp.int32)[None, :]
    return jnp.sum(jnp.where(hit, table[None, :], 0.0), axis=1)


def from_behind(block, axis, distance):
    devices = range(lax.axis_size(axis))
    route = [((i - distance) % len(devices), i) for i in devices]
    return lax.ppermute(block, axis, route)


def flip(block, axis, bits):
    return lax.ppermute(block, axis, [(i, i ^ bits) for i in range(lax.axis_size(axis))])


def contribute(full_rows, panel_rows, w_mat, nu_val, weight_val, energies, omega_grid, n_dev):
    product = jnp.dot(full_rows, w_mat, preferred_element_type=jnp.float32)
    contract = jnp.sum(product * panel_rows.astype(jnp.float32), axis=-1).reshape(n_dev, -1)
    offsets = omega_grid[None, :] - energies[:, None]
    kernel = offsets / (offsets * offsets + nu_val * nu_val)
    return -weight_val / math.pi * jnp.dot(contract, kernel, precision=lax.Precision.HIGHEST)


def general(pair_matrix, screened, imag_freq, quad_weight, band_energy, band_index):
    n_dev, m_dev, g_panel = pair_matrix.shape
    f_dev = screened.shape[0]
    cycle_size = lax.axis_size("freq")
    cycle_pos = lax.axis_index("freq")
    full_pairs = lax.all_gather(pair_matrix, "ga", axis=2, tiled=True)
    g_all = full_pairs.shape[2]
    omega_grid = make_grid(NW)
    sigma_part = jnp.zeros((n_dev, NW), jnp.float32)
    panel_rows = pair_matrix.reshape(n_dev * m_dev, g_panel)
    full_rows = full_pairs.reshape(n_dev * m_dev, g_all)
    energies = lookup(band_index, band_energy)
    nu_all = lax.all_gather(imag_freq, "freq", axis=0, tiled=True)
    weight_all = lax.all_gather(quad_weight, "freq", axis=0, tiled=True)
    w_slab = screened
    for turn_index in range(cycle_size):
        source = jnp.mod(cycle_pos - turn_index, cycle_size)
        nu_vals = lax.dynamic_slice_in_dim(nu_all, source * f_dev, f_dev)
        weight_vals = lax.dynamic_slice_in_dim(weight_all, source * f_dev, f_dev)
        for slot in range(f_dev):
            sigma_part = sigma_part + contribute(
                full_rows, panel_rows, w_slab[slot], nu_vals[slot], weight_vals[slot],
                energies, omega_grid, n_dev,
            )
        if turn_index + 1 < cycle_size:
            w_slab = from_behind(w_slab, "freq", 1)
    return lax.psum(sigma_part, ("freq", "ga"))


def choose(flag, yes, no):
    @pl.when(flag == 1)
    def _():
        yes.start()

    @pl.when(flag == 0)
    def _():
        no.start()


def start_slot(plan, slot, where_ref, refs, w_all, w_sems):
    at = 0
    for index, lead, begin, count in plan[slot]:
        if lead is None:
            src = refs[index].at[begin : begin + count, :]
        elif begin is None:
            src = refs[index].at[where_ref[5 + lead]]
        else:
            src = refs[index].at[where_ref[lead], pl.ds(pl.multiple_of(where_ref[begin], count // 2), count), :]
        pltpu.make_async_copy(src, w_all.at[slot, at : at + count, :], w_sems.at[slot]).start()
        at += count


def quadratic_kernel(plan, m_dev, tile, kind, where_ref, k_ref, own_ref, a_ref, b_ref, *rest):
    refs = rest[: len(rest) - 7]
    out_ref, left, right, w_all, k_all, sems, w_sems = rest[len(rest) - 7 :]
    n_slots, _, panel = w_all.shape
    end, low = where_ref[0], where_ref[1]
    if kind == "near":
        w_refs = refs
        here = left.at[:, pl.ds(pl.multiple_of((1 - low) * panel, panel), panel)]
        there = left.at[:, pl.ds(pl.multiple_of(low * panel, panel), panel)]
        fixed = [(own_ref, here), (own_ref, right)]
        either = [((a_ref, b_ref), there)]
    else:
        c_ref, w_refs = refs[0], refs[1:]
        fixed = [(a_ref, left.at[:, panel:])]
        either = [((b_ref, own_ref), left.at[:, :panel]), ((own_ref, c_ref), right)]
    start_slot(plan, 0, where_ref, w_refs, w_all, w_sems)
    waits = [pltpu.make_async_copy(src, dst, sems.at[n]) for n, (src, dst) in enumerate(fixed)]
    for c in waits:
        c.start()
    for n, ((yes, no), dst) in enumerate(either):
        sem = sems.at[len(fixed) + n]
        waits.append(pltpu.make_async_copy(yes, dst, sem))
        choose(end, waits[-1], pltpu.make_async_copy(no, dst, sem))
    waits.append(pltpu.make_async_copy(k_ref, k_all, sems.at[4]))
    waits[-1].start()
    for slot in range(1, n_slots):
        start_slot(plan, slot, where_ref, w_refs, w_all, w_sems)
    out_ref[...] = jnp.zeros_like(out_ref)
    for c in waits:
        c.wait()

    def one(slot, carry):
        pltpu.make_async_copy(w_all.at[slot], w_all.at[slot], w_sems.at[slot]).wait()
        for t in range(right.shape[0] // tile):
            at = slice(t * tile, (t + 1) * tile)
            y = jnp.dot(left[at], w_all[slot], preferred_element_type=jnp.float32)
            c = jnp.sum(y * right[at].astype(jnp.float32), axis=1, keepdims=True)
            for k in range(tile // m_dev):
                term = c[k * m_dev : (k + 1) * m_dev] * k_all[slot]
                out_ref[t * (tile // m_dev) + k] += jnp.sum(term.reshape(m_dev // 8, 8, NW), axis=0)
        return carry

    lax.fori_loop(0, n_slots, one, 0)


def turn_kernel(where_ref, far_ref, given_ref, out_ref):
    panel = far_ref.shape[0]

    @pl.when(where_ref[0] == 1)
    def _():
        out_ref[:panel] = far_ref[...]

    @pl.when(where_ref[0] == 0)
    def _():
        out_ref[:panel] = far_ref[...].T

    out_ref[panel:] = given_ref[...].T


def run_kernel(kind, plan, where, k_part, mats, arrays, m_dev):
    n_rows, panel = mats[0].shape
    n_slots, depth = k_part.shape[0], 2 * panel
    scratch = [
        pltpu.VMEM((n_rows, depth), jnp.bfloat16),
        pltpu.VMEM((n_rows, panel), jnp.bfloat16),
        pltpu.VMEM((n_slots, depth, panel), jnp.bfloat16),
        pltpu.VMEM(k_part.shape, jnp.float32),
        pltpu.SemaphoreType.DMA((5,)),
        pltpu.SemaphoreType.DMA((n_slots,)),
    ]
    flops = 2 * n_rows * depth * panel * n_slots
    return pl.pallas_call(
        functools.partial(quadratic_kernel, plan, m_dev, n_rows // 2, kind),
        out_shape=jax.ShapeDtypeStruct((n_rows // m_dev, 8, NW), jnp.float32),
        in_specs=[pl.BlockSpec(memory_space=pltpu.SMEM)]
        + [pl.BlockSpec(memory_space=pl.ANY)] * (1 + len(mats) + len(arrays)),
        out_specs=pl.BlockSpec(memory_space=pltpu.VMEM),
        scratch_shapes=scratch,
        cost_estimate=pl.CostEstimate(flops=flops, bytes_accessed=depth * panel, transcendentals=0),
        compiler_params=pltpu.CompilerParams(vmem_limit_bytes=48 * 2**20),
    )(where, k_part, *mats, *arrays)


def split3(x):
    hi = lax.reduce_precision(x, 8, 7)
    mid = lax.reduce_precision(x - hi, 8, 7)
    return jnp.stack([hi, mid, (x - hi) - mid])


def after(value, *others):
    return lax.optimization_barrier((value,) + others)[0]


def square_line(pair_matrix, screened, imag_freq, quad_weight, band_energy, band_index):
    n_dev, m_dev, panel = pair_matrix.shape
    ga = lax.axis_index("ga")
    core = lax.axis_index("band")
    rows = n_dev * m_dev
    own = pair_matrix.reshape(rows, panel)
    end = (ga == 0) | (ga == 3)
    low = ga < 2
    near_at = jnp.where(ga == 0, 0, jnp.where(ga == 3, 2, 1)) * panel
    far_at = (ga + 2) % 4 * panel
    give_at = jnp.where(ga % 2 == 0, 3, 0) * panel
    where = jnp.stack([end, low, near_at, core, 1 - core]).astype(jnp.int32)

    outer = [(0, 1), (1, 0), (2, 3), (3, 2)]
    inner = [(1, 2), (2, 1)]
    outward = [(1, 0), (2, 3)]

    def piece(start, count):
        return lax.dynamic_slice(screened, (core, start, 0), (1, count, panel))[0]

    def share(block):
        return flip(block, "band", 1)

    given = lax.ppermute(piece(give_at, panel), "ga", outer)
    node = split3(jnp.stack([imag_freq[core], quad_weight[core]])).reshape(1, 6)
    node = jnp.pad(node, ((0, 15), (0, panel - 6))).astype(jnp.bfloat16)
    near_w = jnp.concatenate([piece(near_at, 2 * panel), node])
    x1 = flip(near_w, "freq", 1)
    y1 = flip(near_w, "freq", 2)
    b_rows = lax.ppermute(own, "ga", inner)
    a_rows = lax.ppermute(after(own, given), "ga", outer)
    far_w = pl.pallas_call(
        turn_kernel,
        out_shape=jax.ShapeDtypeStruct((2 * panel, panel), jnp.bfloat16),
        in_specs=[pl.BlockSpec(memory_space=pltpu.SMEM)] + [pl.BlockSpec(memory_space=pltpu.VMEM)] * 2,
        out_specs=pl.BlockSpec(memory_space=pltpu.VMEM),
        cost_estimate=pl.CostEstimate(flops=0, bytes_accessed=4 * panel * panel, transcendentals=0),
    )(where, piece(far_at, panel), given)
    far_all = lax.all_gather(far_w, ("freq", "band"))
    d1a = flip(y1[:panel], "freq", 1)
    d1b = flip(x1[panel:], "freq", 2)
    x1_o, y1_o, d1a_o, d1b_o = share(x1), share(y1), share(d1a), share(d1b)
    c_rows = lax.ppermute(b_rows, "ga", outward)
    d_rows = lax.ppermute(a_rows, "ga", inner)

    energies = lookup(band_index, band_energy)
    offsets = make_grid(NW)[None, :] - energies[:, None]
    mine = jnp.stack([imag_freq, quad_weight], axis=1)
    mine = jnp.where(core == 0, mine, mine[::-1])

    def weigh(nodes):
        nu, weight = nodes[:, 0, None, None], nodes[:, 1, None, None]
        return (-weight / math.pi) * (offsets / (offsets * offsets + nu * nu))

    def carried(*places):
        terms = jnp.stack([w[row, :6] for w, row in places]).astype(jnp.float32).reshape(-1, 3, 2)
        return (terms[:, 0] + terms[:, 1]) + terms[:, 2]

    here = jnp.concatenate([mine, carried((x1, 2 * panel), (y1, 2 * panel))])
    there = carried((x1_o, 2 * panel), (y1_o, 2 * panel), (d1b, panel), (d1b_o, panel))
    k_here, k_there = weigh(here), weigh(there)
    k_all = jnp.concatenate([k_here, k_there])

    whole, one = 2 * panel, panel
    first = [[(0, 3 + s, 2, whole)] for s in range(2)] + [[(r, None, 0, whole)] for r in (1, 2)]
    second = [[(r, None, 0, whole)] for r in (0, 1)]
    second += [[(r, None, 0, one), (r + 1, None, 0, one)] for r in (2, 4)]
    panels = (own, a_rows, b_rows)
    near = run_kernel("near", first, where, k_here, panels, (screened, x1, y1), m_dev)
    near += run_kernel("near", second, where, k_there, panels, (x1_o, y1_o, d1a, d1b, d1a_o, d1b_o), m_dev)

    square = lax.axis_index("freq")
    order = ((0, core), (0, 1 - core), (1, core), (2, core), (1, 1 - core), (2, 1 - core), (3, core), (3, 1 - core))
    ranks = jnp.stack([(square ^ r) * 2 + c for r, c in order]).astype(jnp.int32)
    far = run_kernel(
        "far", [[(0, n, None, whole)] for n in range(8)], jnp.concatenate([where, ranks]), k_all,
        (own, a_rows, c_rows), (d_rows, far_all), m_dev,
    )
    sigma = jnp.sum(near + far, axis=1)
    for axis in ("freq", "ga"):
        t1, t2, t3 = (flip(sigma, axis, r) for r in (1, 2, 3))
        sigma = (sigma + t1) + (t2 + t3)
    return sigma


def on_device(pair_matrix, screened, *rest):
    sizes = tuple(lax.axis_size(a) for a in ("freq", "ga", "band"))
    fits = sizes == (4, 4, 2) and screened.shape[0] == 2 and pair_matrix.shape[0] % 8 == 0
    return (square_line if fits else general)(pair_matrix, screened, *rest)


def solution(mesh):
    placed = (P("band", "freq", "ga"), P("freq", None, "ga"), P("freq"), P("freq"), P(), P("freq"))
    return jax.shard_map(
        on_device, mesh=mesh, in_specs=placed, out_specs=P("band", None), check_vma=False
    )
```

```python
import functools
import math

import jax
import jax.numpy as jnp
from jax import lax
from jax.experimental import pallas as pl
from jax.experimental.pallas import tpu as pltpu
from jax.sharding import PartitionSpec as P

NW = 256

omega_low = -10.0
omega_span = 20.0


def make_grid(count):
    return omega_low + omega_span * jnp.arange(count, dtype=jnp.float32) / (count - 1)


def lookup(indices, table):
    hit = indices[:, None] == jnp.arange(table.shape[0], dtype=jnp.int32)[None, :]
    return jnp.sum(jnp.where(hit, table[None, :], 0.0), axis=1)


def from_behind(block, axis, distance):
    devices = range(lax.axis_size(axis))
    route = [((i - distance) % len(devices), i) for i in devices]
    return lax.ppermute(block, axis, route)


def flip(block, axis, bits):
    return lax.ppermute(block, axis, [(i, i ^ bits) for i in range(lax.axis_size(axis))])


def contribute(full_rows, panel_rows, w_mat, nu_val, weight_val, energies, omega_grid, n_dev):
    product = jnp.dot(full_rows, w_mat, preferred_element_type=jnp.float32)
    contract = jnp.sum(product * panel_rows.astype(jnp.float32), axis=-1).reshape(n_dev, -1)
    offsets = omega_grid[None, :] - energies[:, None]
    kernel = offsets / (offsets * offsets + nu_val * nu_val)
    return -weight_val / math.pi * jnp.dot(contract, kernel, precision=lax.Precision.HIGHEST)


def general(pair_matrix, screened, imag_freq, quad_weight, band_energy, band_index):
    n_dev, m_dev, g_panel = pair_matrix.shape
    f_dev = screened.shape[0]
    cycle_size = lax.axis_size("freq")
    cycle_pos = lax.axis_index("freq")
    full_pairs = lax.all_gather(pair_matrix, "ga", axis=2, tiled=True)
    g_all = full_pairs.shape[2]
    omega_grid = make_grid(NW)
    sigma_part = jnp.zeros((n_dev, NW), jnp.float32)
    panel_rows = pair_matrix.reshape(n_dev * m_dev, g_panel)
    full_rows = full_pairs.reshape(n_dev * m_dev, g_all)
    energies = lookup(band_index, band_energy)
    nu_all = lax.all_gather(imag_freq, "freq", axis=0, tiled=True)
    weight_all = lax.all_gather(quad_weight, "freq", axis=0, tiled=True)
    w_slab = screened
    for turn_index in range(cycle_size):
        source = jnp.mod(cycle_pos - turn_index, cycle_size)
        nu_vals = lax.dynamic_slice_in_dim(nu_all, source * f_dev, f_dev)
        weight_vals = lax.dynamic_slice_in_dim(weight_all, source * f_dev, f_dev)
        for slot in range(f_dev):
            sigma_part = sigma_part + contribute(
                full_rows, panel_rows, w_slab[slot], nu_vals[slot], weight_vals[slot],
                energies, omega_grid, n_dev,
            )
        if turn_index + 1 < cycle_size:
            w_slab = from_behind(w_slab, "freq", 1)
    return lax.psum(sigma_part, ("freq", "ga"))


def choose(flag, yes, no):
    @pl.when(flag == 1)
    def _():
        yes.start()

    @pl.when(flag == 0)
    def _():
        no.start()


def start_slot(plan, slot, where_ref, refs, w_all, w_sems):
    at = 0
    for index, lead, begin, count in plan[slot]:
        src = refs[index]
        if lead is not None:
            src = src.at[where_ref[lead[1]] if isinstance(lead, tuple) else lead]
        if isinstance(begin, tuple):
            begin = pl.multiple_of(where_ref[begin[1]], count // 2)
        src = src.at[pl.ds(begin, count), :]
        pltpu.make_async_copy(src, w_all.at[slot, at : at + count, :], w_sems.at[slot]).start()
        at += count


def quadratic_kernel(plan, m_dev, begin, tile, kind, where_ref, k_ref, own_ref, a_ref, b_ref, *rest):
    refs = rest[: len(rest) - 7]
    out_ref, left, right, w_all, k_all, sems, w_sems = rest[len(rest) - 7 :]
    n_slots, _, panel = w_all.shape
    end, low = where_ref[0], where_ref[1]
    own_ref, a_ref = (r.at[begin : begin + right.shape[0], :] for r in (own_ref, a_ref))
    if kind == "near":
        w_refs = refs
        here = left.at[:, pl.ds(pl.multiple_of((1 - low) * panel, panel), panel)]
        there = left.at[:, pl.ds(pl.multiple_of(low * panel, panel), panel)]
        fixed = [(own_ref, here), (own_ref, right)]
        either = [((a_ref, b_ref), there)]
    else:
        c_ref, d_ref, w_refs = refs[0], refs[1], refs[2:]
        fixed = [(a_ref, left.at[:, panel:])]
        either = [((c_ref, own_ref), left.at[:, :panel]), ((own_ref, d_ref), right)]
    start_slot(plan, 0, where_ref, w_refs, w_all, w_sems)
    waits = [pltpu.make_async_copy(src, dst, sems.at[n]) for n, (src, dst) in enumerate(fixed)]
    for c in waits:
        c.start()
    for n, ((yes, no), dst) in enumerate(either):
        sem = sems.at[len(fixed) + n]
        waits.append(pltpu.make_async_copy(yes, dst, sem))
        choose(end, waits[-1], pltpu.make_async_copy(no, dst, sem))
    waits.append(pltpu.make_async_copy(k_ref, k_all, sems.at[5]))
    waits[-1].start()
    for slot in range(1, n_slots):
        start_slot(plan, slot, where_ref, w_refs, w_all, w_sems)
    out_ref[...] = jnp.zeros_like(out_ref)
    for c in waits:
        c.wait()

    def one(slot, carry):
        pltpu.make_async_copy(w_all.at[slot], w_all.at[slot], w_sems.at[slot]).wait()
        for t in range(right.shape[0] // tile):
            at = slice(t * tile, (t + 1) * tile)
            y = jnp.dot(left[at], w_all[slot], preferred_element_type=jnp.float32)
            c = jnp.sum(y * right[at].astype(jnp.float32), axis=1, keepdims=True)
            for k in range(tile // m_dev):
                term = c[k * m_dev : (k + 1) * m_dev] * k_all[slot]
                out_ref[t * (tile // m_dev) + k] += jnp.sum(term.reshape(m_dev // 8, 8, NW), axis=0)
        return carry

    lax.fori_loop(0, n_slots, one, 0)


def turn_kernel(where_ref, blocks_ref, out_ref):
    for n in range(2):
        slot = where_ref[3 + n]

        @pl.when(where_ref[0] == 1)
        def _():
            out_ref[n] = blocks_ref[slot]

        @pl.when(where_ref[0] == 0)
        def _():
            out_ref[n] = blocks_ref[slot].T


def transpose_kernel(block_ref, out_ref):
    out_ref[...] = block_ref[...].T


def run_kernel(kind, plan, where, k_part, mats, arrays, m_dev, begin=0):
    n_rows, panel = mats[0].shape
    n_slots, depth = k_part.shape[0], 2 * panel
    scratch = [
        pltpu.VMEM((n_rows, depth), jnp.bfloat16),
        pltpu.VMEM((n_rows, panel), jnp.bfloat16),
        pltpu.VMEM((n_slots, depth, panel), jnp.bfloat16),
        pltpu.VMEM(k_part.shape, jnp.float32),
        pltpu.SemaphoreType.DMA((6,)),
        pltpu.SemaphoreType.DMA((n_slots,)),
    ]
    flops = 2 * n_rows * depth * panel * n_slots // (16 if kind == "near" else 1)
    return pl.pallas_call(
        functools.partial(quadratic_kernel, plan, m_dev, begin, min(n_rows, 4 * m_dev), kind),
        out_shape=jax.ShapeDtypeStruct((n_rows // m_dev, 8, NW), jnp.float32),
        in_specs=[pl.BlockSpec(memory_space=pltpu.SMEM)]
        + [pl.BlockSpec(memory_space=pl.ANY)] * (1 + len(mats) + len(arrays)),
        out_specs=pl.BlockSpec(memory_space=pltpu.VMEM),
        scratch_shapes=scratch,
        cost_estimate=pl.CostEstimate(flops=flops, bytes_accessed=depth * panel, transcendentals=0),
        compiler_params=pltpu.CompilerParams(vmem_limit_bytes=48 * 2**20),
    )(where, k_part, *mats, *arrays)


def split3(x):
    hi = lax.reduce_precision(x, 8, 7)
    mid = lax.reduce_precision(x - hi, 8, 7)
    return jnp.stack([hi, mid, (x - hi) - mid])


def after(value, *others):
    return lax.optimization_barrier((value,) + others)[0]


def square_line(pair_matrix, screened, imag_freq, quad_weight, band_energy, band_index):
    n_dev, m_dev, panel = pair_matrix.shape
    ga = lax.axis_index("ga")
    core = lax.axis_index("band")
    rows = n_dev * m_dev
    own = pair_matrix.reshape(rows, panel)
    end = (ga == 0) | (ga == 3)
    low = ga < 2
    near_at = jnp.where(ga == 0, 0, jnp.where(ga == 3, 2, 1)) * panel
    far_at = (ga + 2) % 4 * panel
    give_at = jnp.where(ga % 2 == 0, 3, 0) * panel
    where = jnp.stack([end, low, near_at, core, 1 - core]).astype(jnp.int32)

    outer = [(0, 1), (1, 0), (2, 3), (3, 2)]
    inner = [(1, 2), (2, 1)]
    outward = [(1, 0), (2, 3)]

    def piece(start, count):
        return lax.dynamic_slice(screened, (core, start, 0), (1, count, panel))[0]

    def share(block):
        return flip(block, "band", 1)

    given = lax.ppermute(piece(give_at, panel), "ga", outer)
    def local(body, shape, *inputs):
        specs = [pl.BlockSpec(memory_space=pltpu.SMEM if x.dtype == jnp.int32 else pltpu.VMEM) for x in inputs]
        return pl.pallas_call(
            body,
            out_shape=jax.ShapeDtypeStruct(shape, jnp.bfloat16),
            in_specs=specs,
            out_specs=pl.BlockSpec(memory_space=pltpu.VMEM),
            cost_estimate=pl.CostEstimate(flops=0, bytes_accessed=4 * panel * panel, transcendentals=0),
        )(*inputs)

    node = split3(jnp.stack([imag_freq[core], quad_weight[core]])).reshape(1, 6)
    node = jnp.pad(node, ((0, 15), (0, panel - 6))).astype(jnp.bfloat16)
    far_blocks = lax.dynamic_slice(screened, (0, far_at, 0), (2, panel, panel))
    far_self = local(turn_kernel, (2, panel, panel), where, far_blocks)
    sent = jnp.concatenate([piece(near_at, 2 * panel), far_self[0], node])
    cut = 3 * panel // 2
    x1 = flip(sent, "freq", 1)
    y1 = flip(sent, "freq", 2)
    b_rows = lax.ppermute(own, "ga", inner)
    a_rows = lax.ppermute(after(own, given), "ga", outer)
    turned = local(transpose_kernel, (panel, panel), given)
    given_all = lax.all_gather(after(turned, x1, y1, b_rows), ("freq", "band"))
    d1a = flip(y1[:cut], "freq", 1)
    d1b = flip(x1[cut:], "freq", 2)
    energies = lookup(band_index, band_energy)
    offsets = make_grid(NW)[None, :] - energies[:, None]
    mine = jnp.stack([imag_freq, quad_weight], axis=1)
    mine = jnp.where(core == 0, mine, mine[::-1])

    def weigh(nodes):
        nu, weight = nodes[:, 0, None, None], nodes[:, 1, None, None]
        return (-weight / math.pi) * (offsets / (offsets * offsets + nu * nu))

    def carried(*places):
        terms = jnp.stack([w[row, :6] for w, row in places]).astype(jnp.float32).reshape(-1, 3, 2)
        return (terms[:, 0] + terms[:, 1]) + terms[:, 2]

    x1_o, y1_o = share(after(x1, a_rows, b_rows)), share(after(y1, a_rows, b_rows, d1a))
    d1a_o, d1b_o = share(d1a), share(d1b)
    c_rows = lax.ppermute(b_rows, "ga", outward)
    d_rows = lax.ppermute(a_rows, "ga", inner)
    ends = ((x1, 3 * panel), (y1, 3 * panel), (x1_o, 3 * panel), (y1_o, 3 * panel), (d1b, cut), (d1b_o, cut))
    k_all = weigh(jnp.concatenate([mine, carried(*ends)]))

    whole = 2 * panel
    slots = [[(0, ("at", 3 + s), ("at", 2), whole)] for s in range(2)]
    slots += [[(r, None, 0, whole)] for r in (1, 2, 3, 4)]
    slots += [[(r, None, 0, cut), (r + 1, None, 0, whole - cut)] for r in (5, 7)]
    arrays = (screened, x1, y1, x1_o, y1_o, d1a, d1b, d1a_o, d1b_o)
    near = run_kernel("near", slots, where, k_all, (own, a_rows, b_rows), arrays, m_dev)

    square = lax.axis_index("freq")
    order = ((0, core), (0, 1 - core), (1, core), (2, core), (1, 1 - core), (2, 1 - core), (3, core), (3, 1 - core))
    ranks = jnp.stack([(square ^ r) * 2 + c for r, c in order]).astype(jnp.int32)
    sources = [(1, 0, 0), (1, 1, 0)] + [(r, None, whole) for r in (2, 3, 4, 5)] + [(r, None, whole - cut) for r in (6, 7)]
    slots = [[(*src, panel), (0, ("at", 5 + n), 0, panel)] for n, src in enumerate(sources)]
    arrays = (given_all, far_self, x1, y1, x1_o, y1_o, d1b, d1b_o)
    far = run_kernel(
        "far", slots, jnp.concatenate([where, ranks]), k_all,
        (own, a_rows, b_rows), (c_rows, d_rows, *arrays), m_dev,
    )
    sigma = jnp.sum(near + far, axis=1)
    for axis in ("freq", "ga"):
        t1, t2, t3 = (flip(sigma, axis, r) for r in (1, 2, 3))
        sigma = (sigma + t1) + (t2 + t3)
    return sigma


def on_device(pair_matrix, screened, *rest):
    sizes = tuple(lax.axis_size(a) for a in ("freq", "ga", "band"))
    fits = sizes == (4, 4, 2) and screened.shape[0] == 2 and pair_matrix.shape[0] % 8 == 0
    return (square_line if fits else general)(pair_matrix, screened, *rest)


def solution(mesh):
    placed = (P("band", "freq", "ga"), P("freq", None, "ga"), P("freq"), P("freq"), P(), P("freq"))
    return jax.shard_map(
        on_device, mesh=mesh, in_specs=placed, out_specs=P("band", None), check_vma=False
    )
```

```python
import functools
import math

import jax
import jax.numpy as jnp
from jax import lax
from jax.experimental import pallas as pl
from jax.experimental.pallas import tpu as pltpu
from jax.sharding import PartitionSpec as P

NW = 256

omega_low = -10.0
omega_span = 20.0


def make_grid(count):
    return omega_low + omega_span * jnp.arange(count, dtype=jnp.float32) / (count - 1)


def lookup(indices, table):
    hit = indices[:, None] == jnp.arange(table.shape[0], dtype=jnp.int32)[None, :]
    return jnp.sum(jnp.where(hit, table[None, :], 0.0), axis=1)


def from_behind(block, axis, distance):
    devices = range(lax.axis_size(axis))
    route = [((i - distance) % len(devices), i) for i in devices]
    return lax.ppermute(block, axis, route)


def flip(block, axis, bits):
    return lax.ppermute(block, axis, [(i, i ^ bits) for i in range(lax.axis_size(axis))])


def contribute(full_rows, panel_rows, w_mat, nu_val, weight_val, energies, omega_grid, n_dev):
    product = jnp.dot(full_rows, w_mat, preferred_element_type=jnp.float32)
    contract = jnp.sum(product * panel_rows.astype(jnp.float32), axis=-1).reshape(n_dev, -1)
    offsets = omega_grid[None, :] - energies[:, None]
    kernel = offsets / (offsets * offsets + nu_val * nu_val)
    return -weight_val / math.pi * jnp.dot(contract, kernel, precision=lax.Precision.HIGHEST)


def general(pair_matrix, screened, imag_freq, quad_weight, band_energy, band_index):
    n_dev, m_dev, g_panel = pair_matrix.shape
    f_dev = screened.shape[0]
    cycle_size = lax.axis_size("freq")
    cycle_pos = lax.axis_index("freq")
    full_pairs = lax.all_gather(pair_matrix, "ga", axis=2, tiled=True)
    g_all = full_pairs.shape[2]
    omega_grid = make_grid(NW)
    sigma_part = jnp.zeros((n_dev, NW), jnp.float32)
    panel_rows = pair_matrix.reshape(n_dev * m_dev, g_panel)
    full_rows = full_pairs.reshape(n_dev * m_dev, g_all)
    energies = lookup(band_index, band_energy)
    nu_all = lax.all_gather(imag_freq, "freq", axis=0, tiled=True)
    weight_all = lax.all_gather(quad_weight, "freq", axis=0, tiled=True)
    w_slab = screened
    for turn_index in range(cycle_size):
        source = jnp.mod(cycle_pos - turn_index, cycle_size)
        nu_vals = lax.dynamic_slice_in_dim(nu_all, source * f_dev, f_dev)
        weight_vals = lax.dynamic_slice_in_dim(weight_all, source * f_dev, f_dev)
        for slot in range(f_dev):
            sigma_part = sigma_part + contribute(
                full_rows, panel_rows, w_slab[slot], nu_vals[slot], weight_vals[slot],
                energies, omega_grid, n_dev,
            )
        if turn_index + 1 < cycle_size:
            w_slab = from_behind(w_slab, "freq", 1)
    return lax.psum(sigma_part, ("freq", "ga"))


def choose(flag, yes, no):
    @pl.when(flag == 1)
    def _():
        yes.start()

    @pl.when(flag == 0)
    def _():
        no.start()


def start_slot(plan, slot, where_ref, refs, w_all, w_sems):
    at = 0
    for index, lead, begin, count in plan[slot]:
        src = refs[index]
        if lead is not None:
            src = src.at[where_ref[lead[1]] if isinstance(lead, tuple) else lead]
        if isinstance(begin, tuple):
            begin = pl.multiple_of(where_ref[begin[1]], count // 2)
        src = src.at[pl.ds(begin, count), :]
        pltpu.make_async_copy(src, w_all.at[slot, at : at + count, :], w_sems.at[slot]).start()
        at += count


def quadratic_kernel(plan, m_dev, begin, tile, kind, where_ref, k_ref, own_ref, a_ref, b_ref, *rest):
    refs = rest[: len(rest) - 7]
    out_ref, left, right, w_all, k_all, sems, w_sems = rest[len(rest) - 7 :]
    n_slots, _, panel = w_all.shape
    end, low = where_ref[0], where_ref[1]
    own_ref, a_ref = (r.at[begin : begin + right.shape[0], :] for r in (own_ref, a_ref))
    if kind == "near":
        w_refs = refs
        here = left.at[:, pl.ds(pl.multiple_of((1 - low) * panel, panel), panel)]
        there = left.at[:, pl.ds(pl.multiple_of(low * panel, panel), panel)]
        fixed = [(own_ref, here), (own_ref, right)]
        either = [((a_ref, b_ref), there)]
    else:
        c_ref, d_ref, w_refs = refs[0], refs[1], refs[2:]
        fixed = [(a_ref, left.at[:, panel:])]
        either = [((c_ref, own_ref), left.at[:, :panel]), ((own_ref, d_ref), right)]
    start_slot(plan, 0, where_ref, w_refs, w_all, w_sems)
    waits = [pltpu.make_async_copy(src, dst, sems.at[n]) for n, (src, dst) in enumerate(fixed)]
    for c in waits:
        c.start()
    for n, ((yes, no), dst) in enumerate(either):
        sem = sems.at[len(fixed) + n]
        waits.append(pltpu.make_async_copy(yes, dst, sem))
        choose(end, waits[-1], pltpu.make_async_copy(no, dst, sem))
    waits.append(pltpu.make_async_copy(k_ref, k_all, sems.at[5]))
    waits[-1].start()
    for slot in range(1, n_slots):
        start_slot(plan, slot, where_ref, w_refs, w_all, w_sems)
    out_ref[...] = jnp.zeros_like(out_ref)
    for c in waits:
        c.wait()

    def one(slot, carry):
        pltpu.make_async_copy(w_all.at[slot], w_all.at[slot], w_sems.at[slot]).wait()
        for t in range(right.shape[0] // tile):
            at = slice(t * tile, (t + 1) * tile)
            y = jnp.dot(left[at], w_all[slot], preferred_element_type=jnp.float32)
            c = jnp.sum(y * right[at].astype(jnp.float32), axis=1, keepdims=True)
            for k in range(tile // m_dev):
                term = c[k * m_dev : (k + 1) * m_dev] * k_all[slot]
                out_ref[t * (tile // m_dev) + k] += jnp.sum(term.reshape(m_dev // 8, 8, NW), axis=0)
        return carry

    lax.fori_loop(0, n_slots, one, 0)


def pack_kernel(where_ref, nu_ref, weight_ref, screened_ref, sent_ref, far_ref, blocks, nodes, sems):
    panel = blocks.shape[1]
    core = where_ref[3]
    near_at = pl.multiple_of(where_ref[2], panel)
    far_at = pl.multiple_of(where_ref[5], panel)
    loads = [
        pltpu.make_async_copy(screened_ref.at[where_ref[3 + n], pl.ds(far_at, panel), :], blocks.at[n], sems.at[n])
        for n in range(2)
    ]
    near = pltpu.make_async_copy(
        screened_ref.at[core, pl.ds(near_at, 2 * panel), :], sent_ref.at[: 2 * panel, :], sems.at[2]
    )
    for c in loads:
        c.start()
    near.start()
    lane = lax.broadcasted_iota(jnp.int32, nodes.shape, 1)
    nu = jnp.full(nodes.shape, nu_ref[core], jnp.float32)
    weight = jnp.full(nodes.shape, weight_ref[core], jnp.float32)
    rest = jnp.where(lane % 2 == 0, nu, weight)
    packed = jnp.zeros(nodes.shape, jnp.float32)
    for n in range(3):
        term = rest.astype(jnp.bfloat16).astype(jnp.float32)
        packed = jnp.where(lane // 2 == n, term, packed)
        rest = rest - term
    nodes[...] = packed.astype(jnp.bfloat16)
    stores = [
        pltpu.make_async_copy(far_ref.at[0], sent_ref.at[2 * panel : 3 * panel, :], sems.at[3]),
        pltpu.make_async_copy(nodes, sent_ref.at[3 * panel :, :], sems.at[4]),
    ]
    stores[1].start()
    for n in range(2):
        loads[n].wait()

        @pl.when(where_ref[0] == 1)
        def _():
            far_ref[n] = blocks[n]

        @pl.when(where_ref[0] == 0)
        def _():
            far_ref[n] = blocks[n].T

        if n == 0:
            stores[0].start()
    for c in stores + [near]:
        c.wait()


def transpose_kernel(block_ref, out_ref):
    out_ref[...] = block_ref[...].T


def run_kernel(kind, plan, where, k_part, mats, arrays, m_dev, begin=0):
    n_rows, panel = mats[0].shape
    n_slots, depth = k_part.shape[0], 2 * panel
    scratch = [
        pltpu.VMEM((n_rows, depth), jnp.bfloat16),
        pltpu.VMEM((n_rows, panel), jnp.bfloat16),
        pltpu.VMEM((n_slots, depth, panel), jnp.bfloat16),
        pltpu.VMEM(k_part.shape, jnp.float32),
        pltpu.SemaphoreType.DMA((6,)),
        pltpu.SemaphoreType.DMA((n_slots,)),
    ]
    flops = 2 * n_rows * depth * panel * n_slots // (16 if kind == "near" else 1)
    return pl.pallas_call(
        functools.partial(quadratic_kernel, plan, m_dev, begin, min(n_rows, 4 * m_dev), kind),
        out_shape=jax.ShapeDtypeStruct((n_rows // m_dev, 8, NW), jnp.float32),
        in_specs=[pl.BlockSpec(memory_space=pltpu.SMEM)]
        + [pl.BlockSpec(memory_space=pl.ANY)] * (1 + len(mats) + len(arrays)),
        out_specs=pl.BlockSpec(memory_space=pltpu.VMEM),
        scratch_shapes=scratch,
        cost_estimate=pl.CostEstimate(flops=flops, bytes_accessed=depth * panel, transcendentals=0),
        compiler_params=pltpu.CompilerParams(vmem_limit_bytes=48 * 2**20),
    )(where, k_part, *mats, *arrays)


def after(value, *others):
    return lax.optimization_barrier((value,) + others)[0]


def square_line(pair_matrix, screened, imag_freq, quad_weight, band_energy, band_index):
    n_dev, m_dev, panel = pair_matrix.shape
    ga = lax.axis_index("ga")
    core = lax.axis_index("band")
    rows = n_dev * m_dev
    own = pair_matrix.reshape(rows, panel)
    end = (ga == 0) | (ga == 3)
    low = ga < 2
    near_at = jnp.where(ga == 0, 0, jnp.where(ga == 3, 2, 1)) * panel
    far_at = (ga + 2) % 4 * panel
    give_at = jnp.where(ga % 2 == 0, 3, 0) * panel
    where = jnp.stack([end, low, near_at, core, 1 - core, far_at]).astype(jnp.int32)

    outer = [(0, 1), (1, 0), (2, 3), (3, 2)]
    inner = [(1, 2), (2, 1)]
    outward = [(1, 0), (2, 3)]

    def piece(start, count):
        return lax.dynamic_slice(screened, (core, start, 0), (1, count, panel))[0]

    def share(block):
        return flip(block, "band", 1)

    given = lax.ppermute(piece(give_at, panel), "ga", outer)
    def local(body, shape, *inputs):
        specs = [pl.BlockSpec(memory_space=pltpu.SMEM if x.dtype == jnp.int32 else pltpu.VMEM) for x in inputs]
        return pl.pallas_call(
            body,
            out_shape=jax.ShapeDtypeStruct(shape, jnp.bfloat16),
            in_specs=specs,
            out_specs=pl.BlockSpec(memory_space=pltpu.VMEM),
            cost_estimate=pl.CostEstimate(flops=0, bytes_accessed=4 * panel * panel, transcendentals=0),
        )(*inputs)

    sent, far_self = pl.pallas_call(
        pack_kernel,
        out_shape=(
            jax.ShapeDtypeStruct((3 * panel + 16, panel), jnp.bfloat16),
            jax.ShapeDtypeStruct((2, panel, panel), jnp.bfloat16),
        ),
        in_specs=[pl.BlockSpec(memory_space=pltpu.SMEM)] * 3 + [pl.BlockSpec(memory_space=pl.ANY)],
        out_specs=(pl.BlockSpec(memory_space=pl.ANY), pl.BlockSpec(memory_space=pltpu.VMEM)),
        scratch_shapes=[
            pltpu.VMEM((2, panel, panel), jnp.bfloat16),
            pltpu.VMEM((16, panel), jnp.bfloat16),
            pltpu.SemaphoreType.DMA((5,)),
        ],
        cost_estimate=pl.CostEstimate(flops=0, bytes_accessed=8 * panel * panel, transcendentals=0),
        compiler_params=pltpu.CompilerParams(vmem_limit_bytes=32 * 2**20),
    )(where, imag_freq, quad_weight, screened)
    cut = 3 * panel // 2
    x1 = flip(sent, "freq", 1)
    y1 = flip(sent, "freq", 2)
    b_rows = lax.ppermute(own, "ga", inner)
    a_rows = lax.ppermute(after(own, given), "ga", outer)
    turned = local(transpose_kernel, (panel, panel), given)
    given_all = lax.all_gather(after(turned, x1, y1, a_rows, b_rows), ("freq", "band"))
    d1a = flip(y1[:cut], "freq", 1)
    d1b = flip(x1[cut:], "freq", 2)
    energies = lookup(band_index, band_energy)
    offsets = make_grid(NW)[None, :] - energies[:, None]
    mine = jnp.stack([imag_freq, quad_weight], axis=1)
    mine = jnp.where(core == 0, mine, mine[::-1])

    def weigh(nodes):
        nu, weight = nodes[:, 0, None, None], nodes[:, 1, None, None]
        return (-weight / math.pi) * (offsets / (offsets * offsets + nu * nu))

    def carried(*places):
        terms = jnp.stack([w[row, :6] for w, row in places]).astype(jnp.float32).reshape(-1, 3, 2)
        return (terms[:, 0] + terms[:, 1]) + terms[:, 2]

    x1_o, y1_o = share(after(x1, a_rows, b_rows)), share(after(y1, a_rows, b_rows, d1a))
    d1a_o, d1b_o = share(d1a), share(d1b)
    c_rows = lax.ppermute(b_rows, "ga", outward)
    d_rows = lax.ppermute(a_rows, "ga", inner)
    ends = ((x1, 3 * panel), (y1, 3 * panel), (x1_o, 3 * panel), (y1_o, 3 * panel), (d1b, cut), (d1b_o, cut))
    k_all = weigh(jnp.concatenate([mine, carried(*ends)]))

    whole = 2 * panel
    slots = [[(0, ("at", 3 + s), ("at", 2), whole)] for s in range(2)]
    slots += [[(r, None, 0, whole)] for r in (1, 2, 3, 4)]
    slots += [[(r, None, 0, cut), (r + 1, None, 0, whole - cut)] for r in (5, 7)]
    arrays = (screened, x1, y1, x1_o, y1_o, d1a, d1b, d1a_o, d1b_o)
    near = run_kernel("near", slots, where, k_all, (own, a_rows, b_rows), arrays, m_dev)

    square = lax.axis_index("freq")
    order = ((0, core), (0, 1 - core), (1, core), (2, core), (1, 1 - core), (2, 1 - core), (3, core), (3, 1 - core))
    ranks = jnp.stack([(square ^ r) * 2 + c for r, c in order]).astype(jnp.int32)
    sources = [(1, 0, 0), (1, 1, 0)] + [(r, None, whole) for r in (2, 3, 4, 5)] + [(r, None, whole - cut) for r in (6, 7)]
    slots = [[(*src, panel), (0, ("at", 6 + n), 0, panel)] for n, src in enumerate(sources)]
    arrays = (given_all, far_self, x1, y1, x1_o, y1_o, d1b, d1b_o)
    far = run_kernel(
        "far", slots, jnp.concatenate([where, ranks]), k_all,
        (own, a_rows, b_rows), (c_rows, d_rows, *arrays), m_dev,
    )
    sigma = jnp.sum(near + far, axis=1)
    for axis in ("freq", "ga"):
        t1, t2, t3 = (flip(sigma, axis, r) for r in (1, 2, 3))
        sigma = (sigma + t1) + (t2 + t3)
    return sigma


def on_device(pair_matrix, screened, *rest):
    sizes = tuple(lax.axis_size(a) for a in ("freq", "ga", "band"))
    fits = sizes == (4, 4, 2) and screened.shape[0] == 2 and pair_matrix.shape[0] % 8 == 0
    return (square_line if fits else general)(pair_matrix, screened, *rest)


def solution(mesh):
    placed = (P("band", "freq", "ga"), P("freq", None, "ga"), P("freq"), P("freq"), P(), P("freq"))
    return jax.shard_map(
        on_device, mesh=mesh, in_specs=placed, out_specs=P("band", None), check_vma=False
    )
```

```python
import functools
import math

import jax
import jax.numpy as jnp
from jax import lax
from jax.experimental import pallas as pl
from jax.experimental.pallas import tpu as pltpu
from jax.sharding import PartitionSpec as P

NW = 256

omega_low = -10.0
omega_span = 20.0


def make_grid(count):
    return omega_low + omega_span * jnp.arange(count, dtype=jnp.float32) / (count - 1)


def lookup(indices, table):
    hit = indices[:, None] == jnp.arange(table.shape[0], dtype=jnp.int32)[None, :]
    return jnp.sum(jnp.where(hit, table[None, :], 0.0), axis=1)


def from_behind(block, axis, distance):
    devices = range(lax.axis_size(axis))
    route = [((i - distance) % len(devices), i) for i in devices]
    return lax.ppermute(block, axis, route)


def flip(block, axis, bits):
    return lax.ppermute(block, axis, [(i, i ^ bits) for i in range(lax.axis_size(axis))])


def contribute(full_rows, panel_rows, w_mat, nu_val, weight_val, energies, omega_grid, n_dev):
    product = jnp.dot(full_rows, w_mat, preferred_element_type=jnp.float32)
    contract = jnp.sum(product * panel_rows.astype(jnp.float32), axis=-1).reshape(n_dev, -1)
    offsets = omega_grid[None, :] - energies[:, None]
    kernel = offsets / (offsets * offsets + nu_val * nu_val)
    return -weight_val / math.pi * jnp.dot(contract, kernel, precision=lax.Precision.HIGHEST)


def general(pair_matrix, screened, imag_freq, quad_weight, band_energy, band_index):
    n_dev, m_dev, g_panel = pair_matrix.shape
    f_dev = screened.shape[0]
    cycle_size = lax.axis_size("freq")
    cycle_pos = lax.axis_index("freq")
    full_pairs = lax.all_gather(pair_matrix, "ga", axis=2, tiled=True)
    g_all = full_pairs.shape[2]
    omega_grid = make_grid(NW)
    sigma_part = jnp.zeros((n_dev, NW), jnp.float32)
    panel_rows = pair_matrix.reshape(n_dev * m_dev, g_panel)
    full_rows = full_pairs.reshape(n_dev * m_dev, g_all)
    energies = lookup(band_index, band_energy)
    nu_all = lax.all_gather(imag_freq, "freq", axis=0, tiled=True)
    weight_all = lax.all_gather(quad_weight, "freq", axis=0, tiled=True)
    w_slab = screened
    for turn_index in range(cycle_size):
        source = jnp.mod(cycle_pos - turn_index, cycle_size)
        nu_vals = lax.dynamic_slice_in_dim(nu_all, source * f_dev, f_dev)
        weight_vals = lax.dynamic_slice_in_dim(weight_all, source * f_dev, f_dev)
        for slot in range(f_dev):
            sigma_part = sigma_part + contribute(
                full_rows, panel_rows, w_slab[slot], nu_vals[slot], weight_vals[slot],
                energies, omega_grid, n_dev,
            )
        if turn_index + 1 < cycle_size:
            w_slab = from_behind(w_slab, "freq", 1)
    return lax.psum(sigma_part, ("freq", "ga"))


def choose(flag, yes, no):
    @pl.when(flag == 1)
    def _():
        yes.start()

    @pl.when(flag == 0)
    def _():
        no.start()


def start_slot(plan, slot, where_ref, refs, w_all, w_sems):
    at = 0
    for index, lead, begin, count in plan[slot]:
        src = refs[index]
        if lead is not None:
            src = src.at[where_ref[lead[1]] if isinstance(lead, tuple) else lead]
        if isinstance(begin, tuple):
            begin = pl.multiple_of(where_ref[begin[1]], count // 2)
        src = src.at[pl.ds(begin, count), :]
        pltpu.make_async_copy(src, w_all.at[slot, at : at + count, :], w_sems.at[slot]).start()
        at += count


def quadratic_kernel(plan, m_dev, begin, tile, kind, where_ref, k_ref, own_ref, a_ref, b_ref, *rest):
    refs = rest[: len(rest) - 7]
    out_ref, left, right, w_all, k_all, sems, w_sems = rest[len(rest) - 7 :]
    n_slots, _, panel = w_all.shape
    end, low = where_ref[0], where_ref[1]
    own_ref, a_ref = (r.at[begin : begin + right.shape[0], :] for r in (own_ref, a_ref))
    if kind == "near":
        w_refs = refs
        here = left.at[:, pl.ds(pl.multiple_of((1 - low) * panel, panel), panel)]
        there = left.at[:, pl.ds(pl.multiple_of(low * panel, panel), panel)]
        fixed = [(own_ref, here), (own_ref, right)]
        either = [((a_ref, b_ref), there)]
    else:
        lower, upper, w_refs = refs[:2], refs[2:4], refs[4:]
        half = right.shape[0] // 2
        fixed = [(a_ref, left.at[:, panel:])]
        either = []
        for n in range(2):
            part = slice(n * half, (n + 1) * half)
            mine = own_ref.at[part, :]
            either.append(((lower[n], mine), left.at[part, :panel]))
            either.append(((mine, upper[n]), right.at[part, :]))
    start_slot(plan, 0, where_ref, w_refs, w_all, w_sems)
    waits = [pltpu.make_async_copy(src, dst, sems.at[n]) for n, (src, dst) in enumerate(fixed)]
    for c in waits:
        c.start()
    for n, ((yes, no), dst) in enumerate(either):
        sem = sems.at[len(fixed) + n]
        waits.append(pltpu.make_async_copy(yes, dst, sem))
        choose(end, waits[-1], pltpu.make_async_copy(no, dst, sem))
    waits.append(pltpu.make_async_copy(k_ref, k_all, sems.at[5]))
    waits[-1].start()
    for slot in range(1, n_slots):
        start_slot(plan, slot, where_ref, w_refs, w_all, w_sems)
    out_ref[...] = jnp.zeros_like(out_ref)
    for c in waits:
        c.wait()

    def one(slot, carry):
        pltpu.make_async_copy(w_all.at[slot], w_all.at[slot], w_sems.at[slot]).wait()
        for t in range(right.shape[0] // tile):
            at = slice(t * tile, (t + 1) * tile)
            y = jnp.dot(left[at], w_all[slot], preferred_element_type=jnp.float32)
            c = jnp.sum(y * right[at].astype(jnp.float32), axis=1, keepdims=True)
            for k in range(tile // m_dev):
                term = c[k * m_dev : (k + 1) * m_dev] * k_all[slot]
                out_ref[t * (tile // m_dev) + k] += jnp.sum(term.reshape(m_dev // 8, 8, NW), axis=0)
        return carry

    lax.fori_loop(0, n_slots, one, 0)


def pack_kernel(where_ref, nu_ref, weight_ref, screened_ref, sent_ref, far_ref, blocks, nodes, sems):
    panel = blocks.shape[1]
    core = where_ref[3]
    near_at = pl.multiple_of(where_ref[2], panel)
    far_at = pl.multiple_of(where_ref[5], panel)
    loads = [
        pltpu.make_async_copy(screened_ref.at[where_ref[3 + n], pl.ds(far_at, panel), :], blocks.at[n], sems.at[n])
        for n in range(2)
    ]
    near = pltpu.make_async_copy(
        screened_ref.at[core, pl.ds(near_at, 2 * panel), :], sent_ref.at[: 2 * panel, :], sems.at[2]
    )
    for c in loads:
        c.start()
    near.start()
    lane = lax.broadcasted_iota(jnp.int32, nodes.shape, 1)
    nu = jnp.full(nodes.shape, nu_ref[core], jnp.float32)
    weight = jnp.full(nodes.shape, weight_ref[core], jnp.float32)
    rest = jnp.where(lane % 2 == 0, nu, weight)
    packed = jnp.zeros(nodes.shape, jnp.float32)
    for n in range(3):
        term = rest.astype(jnp.bfloat16).astype(jnp.float32)
        packed = jnp.where(lane // 2 == n, term, packed)
        rest = rest - term
    nodes[...] = packed.astype(jnp.bfloat16)
    stores = [
        pltpu.make_async_copy(far_ref.at[0], sent_ref.at[2 * panel : 3 * panel, :], sems.at[3]),
        pltpu.make_async_copy(nodes, sent_ref.at[3 * panel :, :], sems.at[4]),
    ]
    stores[1].start()
    for n in range(2):
        loads[n].wait()

        @pl.when(where_ref[0] == 1)
        def _():
            far_ref[n] = blocks[n]

        @pl.when(where_ref[0] == 0)
        def _():
            far_ref[n] = blocks[n].T

        if n == 0:
            stores[0].start()
    for c in stores + [near]:
        c.wait()


def transpose_kernel(block_ref, out_ref):
    out_ref[...] = block_ref[...].T


def run_kernel(kind, plan, where, k_part, mats, arrays, m_dev, begin=0):
    n_rows, panel = mats[0].shape
    n_slots, depth = k_part.shape[0], 2 * panel
    scratch = [
        pltpu.VMEM((n_rows, depth), jnp.bfloat16),
        pltpu.VMEM((n_rows, panel), jnp.bfloat16),
        pltpu.VMEM((n_slots, depth, panel), jnp.bfloat16),
        pltpu.VMEM(k_part.shape, jnp.float32),
        pltpu.SemaphoreType.DMA((6,)),
        pltpu.SemaphoreType.DMA((n_slots,)),
    ]
    flops = 2 * n_rows * depth * panel * n_slots // (16 if kind == "near" else 1)
    return pl.pallas_call(
        functools.partial(quadratic_kernel, plan, m_dev, begin, min(n_rows, 4 * m_dev), kind),
        out_shape=jax.ShapeDtypeStruct((n_rows // m_dev, 8, NW), jnp.float32),
        in_specs=[pl.BlockSpec(memory_space=pltpu.SMEM)]
        + [pl.BlockSpec(memory_space=pl.ANY)] * (1 + len(mats) + len(arrays)),
        out_specs=pl.BlockSpec(memory_space=pltpu.VMEM),
        scratch_shapes=scratch,
        cost_estimate=pl.CostEstimate(flops=flops, bytes_accessed=depth * panel, transcendentals=0),
        compiler_params=pltpu.CompilerParams(vmem_limit_bytes=48 * 2**20),
    )(where, k_part, *mats, *arrays)


def after(value, *others):
    return lax.optimization_barrier((value,) + others)[0]


def square_line(pair_matrix, screened, imag_freq, quad_weight, band_energy, band_index):
    n_dev, m_dev, panel = pair_matrix.shape
    ga = lax.axis_index("ga")
    core = lax.axis_index("band")
    rows = n_dev * m_dev
    own = pair_matrix.reshape(rows, panel)
    end = (ga == 0) | (ga == 3)
    low = ga < 2
    near_at = jnp.where(ga == 0, 0, jnp.where(ga == 3, 2, 1)) * panel
    far_at = (ga + 2) % 4 * panel
    give_at = jnp.where(ga % 2 == 0, 3, 0) * panel
    where = jnp.stack([end, low, near_at, core, 1 - core, far_at]).astype(jnp.int32)

    outer = [(0, 1), (1, 0), (2, 3), (3, 2)]
    inner = [(1, 2), (2, 1)]
    outward = [(1, 0), (2, 3)]

    def piece(start, count):
        return lax.dynamic_slice(screened, (core, start, 0), (1, count, panel))[0]

    def share(block):
        return flip(block, "band", 1)

    given = lax.ppermute(piece(give_at, panel), "ga", outer)
    def local(body, shape, *inputs):
        specs = [pl.BlockSpec(memory_space=pltpu.SMEM if x.dtype == jnp.int32 else pltpu.VMEM) for x in inputs]
        return pl.pallas_call(
            body,
            out_shape=jax.ShapeDtypeStruct(shape, jnp.bfloat16),
            in_specs=specs,
            out_specs=pl.BlockSpec(memory_space=pltpu.VMEM),
            cost_estimate=pl.CostEstimate(flops=0, bytes_accessed=4 * panel * panel, transcendentals=0),
        )(*inputs)

    sent, far_self = pl.pallas_call(
        pack_kernel,
        out_shape=(
            jax.ShapeDtypeStruct((3 * panel + 16, panel), jnp.bfloat16),
            jax.ShapeDtypeStruct((2, panel, panel), jnp.bfloat16),
        ),
        in_specs=[pl.BlockSpec(memory_space=pltpu.SMEM)] * 3 + [pl.BlockSpec(memory_space=pl.ANY)],
        out_specs=(pl.BlockSpec(memory_space=pl.ANY), pl.BlockSpec(memory_space=pltpu.VMEM)),
        scratch_shapes=[
            pltpu.VMEM((2, panel, panel), jnp.bfloat16),
            pltpu.VMEM((16, panel), jnp.bfloat16),
            pltpu.SemaphoreType.DMA((5,)),
        ],
        cost_estimate=pl.CostEstimate(flops=0, bytes_accessed=8 * panel * panel, transcendentals=0),
        compiler_params=pltpu.CompilerParams(vmem_limit_bytes=32 * 2**20),
    )(where, imag_freq, quad_weight, screened)
    cut = 3 * panel // 2
    x1 = flip(sent, "freq", 1)
    y1 = flip(sent, "freq", 2)
    b_rows = lax.ppermute(own, "ga", inner)
    a_rows = lax.ppermute(after(own, given), "ga", outer)
    turned = local(transpose_kernel, (panel, panel), given)
    given_all = lax.all_gather(after(turned, x1, y1, a_rows, b_rows), ("freq", "band"))
    d1a = flip(y1[:cut], "freq", 1)
    d1b = flip(x1[cut:], "freq", 2)
    energies = lookup(band_index, band_energy)
    offsets = make_grid(NW)[None, :] - energies[:, None]
    mine = jnp.stack([imag_freq, quad_weight], axis=1)
    mine = jnp.where(core == 0, mine, mine[::-1])

    def weigh(nodes):
        nu, weight = nodes[:, 0, None, None], nodes[:, 1, None, None]
        return (-weight / math.pi) * (offsets / (offsets * offsets + nu * nu))

    def carried(*places):
        terms = jnp.stack([w[row, :6] for w, row in places]).astype(jnp.float32).reshape(-1, 3, 2)
        return (terms[:, 0] + terms[:, 1]) + terms[:, 2]

    half = rows // 2
    c_rows = [lax.ppermute(b_rows[:half], "ga", outward)]
    d_rows = [lax.ppermute(a_rows[:half], "ga", inner)]
    c_rows.append(lax.ppermute(after(b_rows[half:], d_rows[0], d1a, d1b), "ga", outward))
    d_rows.append(lax.ppermute(after(a_rows[half:], c_rows[0], d1a, d1b), "ga", inner))
    x1_o, y1_o, d1a_o, d1b_o = (share(after(w, c_rows[0], d_rows[0], d1a, d1b)) for w in (x1, y1, d1a, d1b))
    ends = ((x1, 3 * panel), (y1, 3 * panel), (x1_o, 3 * panel), (y1_o, 3 * panel), (d1b, cut), (d1b_o, cut))
    k_all = weigh(jnp.concatenate([mine, carried(*ends)]))

    whole = 2 * panel
    slots = [[(0, ("at", 3 + s), ("at", 2), whole)] for s in range(2)]
    slots += [[(r, None, 0, whole)] for r in (1, 2, 3, 4)]
    slots += [[(r, None, 0, cut), (r + 1, None, 0, whole - cut)] for r in (5, 7)]
    arrays = (screened, x1, y1, x1_o, y1_o, d1a, d1b, d1a_o, d1b_o)
    near = run_kernel("near", slots, where, k_all, (own, a_rows, b_rows), arrays, m_dev)

    square = lax.axis_index("freq")
    order = ((0, core), (0, 1 - core), (1, core), (2, core), (1, 1 - core), (2, 1 - core), (3, core), (3, 1 - core))
    ranks = jnp.stack([(square ^ r) * 2 + c for r, c in order]).astype(jnp.int32)
    sources = [(1, 0, 0), (1, 1, 0)] + [(r, None, whole) for r in (2, 3, 4, 5)] + [(r, None, whole - cut) for r in (6, 7)]
    slots = [[(*src, panel), (0, ("at", 6 + n), 0, panel)] for n, src in enumerate(sources)]
    arrays = (given_all, far_self, x1, y1, x1_o, y1_o, d1b, d1b_o)
    far = run_kernel(
        "far", slots, jnp.concatenate([where, ranks]), k_all,
        (own, a_rows, b_rows), (*c_rows, *d_rows, *arrays), m_dev,
    )
    sigma = jnp.sum(near + far, axis=1)
    for axis in ("freq", "ga"):
        t1, t2, t3 = (flip(sigma, axis, r) for r in (1, 2, 3))
        sigma = (sigma + t1) + (t2 + t3)
    return sigma


def on_device(pair_matrix, screened, *rest):
    sizes = tuple(lax.axis_size(a) for a in ("freq", "ga", "band"))
    fits = sizes == (4, 4, 2) and screened.shape[0] == 2 and pair_matrix.shape[0] % 8 == 0
    return (square_line if fits else general)(pair_matrix, screened, *rest)


def solution(mesh):
    placed = (P("band", "freq", "ga"), P("freq", None, "ga"), P("freq"), P("freq"), P(), P("freq"))
    return jax.shard_map(
        on_device, mesh=mesh, in_specs=placed, out_specs=P("band", None), check_vma=False
    )
```

```python
import functools
import math

import jax
import jax.numpy as jnp
from jax import lax
from jax.experimental import pallas as pl
from jax.experimental.pallas import tpu as pltpu
from jax.sharding import PartitionSpec as P

NW = 256

omega_low = -10.0
omega_span = 20.0


def make_grid(count):
    return omega_low + omega_span * jnp.arange(count, dtype=jnp.float32) / (count - 1)


def lookup(indices, table):
    hit = indices[:, None] == jnp.arange(table.shape[0], dtype=jnp.int32)[None, :]
    return jnp.sum(jnp.where(hit, table[None, :], 0.0), axis=1)


def from_behind(block, axis, distance):
    devices = range(lax.axis_size(axis))
    route = [((i - distance) % len(devices), i) for i in devices]
    return lax.ppermute(block, axis, route)


def flip(block, axis, bits):
    return lax.ppermute(block, axis, [(i, i ^ bits) for i in range(lax.axis_size(axis))])


def contribute(full_rows, panel_rows, w_mat, nu_val, weight_val, energies, omega_grid, n_dev):
    product = jnp.dot(full_rows, w_mat, preferred_element_type=jnp.float32)
    contract = jnp.sum(product * panel_rows.astype(jnp.float32), axis=-1).reshape(n_dev, -1)
    offsets = omega_grid[None, :] - energies[:, None]
    kernel = offsets / (offsets * offsets + nu_val * nu_val)
    return -weight_val / math.pi * jnp.dot(contract, kernel, precision=lax.Precision.HIGHEST)


def general(pair_matrix, screened, imag_freq, quad_weight, band_energy, band_index):
    n_dev, m_dev, g_panel = pair_matrix.shape
    f_dev = screened.shape[0]
    cycle_size = lax.axis_size("freq")
    cycle_pos = lax.axis_index("freq")
    full_pairs = lax.all_gather(pair_matrix, "ga", axis=2, tiled=True)
    g_all = full_pairs.shape[2]
    omega_grid = make_grid(NW)
    sigma_part = jnp.zeros((n_dev, NW), jnp.float32)
    panel_rows = pair_matrix.reshape(n_dev * m_dev, g_panel)
    full_rows = full_pairs.reshape(n_dev * m_dev, g_all)
    energies = lookup(band_index, band_energy)
    nu_all = lax.all_gather(imag_freq, "freq", axis=0, tiled=True)
    weight_all = lax.all_gather(quad_weight, "freq", axis=0, tiled=True)
    w_slab = screened
    for turn_index in range(cycle_size):
        source = jnp.mod(cycle_pos - turn_index, cycle_size)
        nu_vals = lax.dynamic_slice_in_dim(nu_all, source * f_dev, f_dev)
        weight_vals = lax.dynamic_slice_in_dim(weight_all, source * f_dev, f_dev)
        for slot in range(f_dev):
            sigma_part = sigma_part + contribute(
                full_rows, panel_rows, w_slab[slot], nu_vals[slot], weight_vals[slot],
                energies, omega_grid, n_dev,
            )
        if turn_index + 1 < cycle_size:
            w_slab = from_behind(w_slab, "freq", 1)
    return lax.psum(sigma_part, ("freq", "ga"))


def choose(flag, yes, no):
    @pl.when(flag == 1)
    def _():
        yes.start()

    @pl.when(flag == 0)
    def _():
        no.start()


def start_slot(plan, slot, where_ref, refs, w_all, w_sems):
    at = 0
    for index, lead, begin, count in plan[slot]:
        src = refs[index]
        if lead is not None:
            src = src.at[where_ref[lead[1]] if isinstance(lead, tuple) else lead]
        if isinstance(begin, tuple):
            begin = pl.multiple_of(where_ref[begin[1]], count // 2)
        src = src.at[pl.ds(begin, count), :]
        pltpu.make_async_copy(src, w_all.at[slot, at : at + count, :], w_sems.at[slot]).start()
        at += count


def quadratic_kernel(plan, m_dev, begin, tile, kind, where_ref, k_ref, own_ref, a_ref, b_ref, *rest):
    refs = rest[: len(rest) - 7]
    out_ref, left, right, w_all, k_all, sems, w_sems = rest[len(rest) - 7 :]
    n_slots, _, panel = w_all.shape
    end, low = where_ref[0], where_ref[1]
    own_ref, a_ref = (r.at[begin : begin + right.shape[0], :] for r in (own_ref, a_ref))
    if kind == "near":
        w_refs = refs
        here = left.at[:, pl.ds(pl.multiple_of((1 - low) * panel, panel), panel)]
        there = left.at[:, pl.ds(pl.multiple_of(low * panel, panel), panel)]
        fixed = [(own_ref, here), (own_ref, right)]
        either = [((a_ref, b_ref), there)]
    else:
        c_ref, d_ref, w_refs = refs[0], refs[1], refs[2:]
        fixed = [(a_ref, left.at[:, panel:])]
        either = [((c_ref, own_ref), left.at[:, :panel]), ((own_ref, d_ref), right)]
    start_slot(plan, 0, where_ref, w_refs, w_all, w_sems)
    waits = [pltpu.make_async_copy(src, dst, sems.at[n]) for n, (src, dst) in enumerate(fixed)]
    for c in waits:
        c.start()
    for n, ((yes, no), dst) in enumerate(either):
        sem = sems.at[len(fixed) + n]
        waits.append(pltpu.make_async_copy(yes, dst, sem))
        choose(end, waits[-1], pltpu.make_async_copy(no, dst, sem))
    waits.append(pltpu.make_async_copy(k_ref, k_all, sems.at[5]))
    waits[-1].start()
    for slot in range(1, n_slots):
        start_slot(plan, slot, where_ref, w_refs, w_all, w_sems)
    out_ref[...] = jnp.zeros_like(out_ref)
    for c in waits:
        c.wait()

    def one(slot, carry):
        pltpu.make_async_copy(w_all.at[slot], w_all.at[slot], w_sems.at[slot]).wait()
        for t in range(right.shape[0] // tile):
            at = slice(t * tile, (t + 1) * tile)
            y = jnp.dot(left[at], w_all[slot], preferred_element_type=jnp.float32)
            c = jnp.sum(y * right[at].astype(jnp.float32), axis=1, keepdims=True)
            for k in range(tile // m_dev):
                term = c[k * m_dev : (k + 1) * m_dev] * k_all[slot]
                out_ref[t * (tile // m_dev) + k] += jnp.sum(term.reshape(m_dev // 8, 8, NW), axis=0)
        return carry

    lax.fori_loop(0, n_slots, one, 0)


def pack_kernel(where_ref, nu_ref, weight_ref, screened_ref, sent_ref, far_ref, blocks, nodes, sems):
    panel = blocks.shape[1]
    core = where_ref[3]
    near_at = pl.multiple_of(where_ref[2], panel)
    far_at = pl.multiple_of(where_ref[5], panel)
    loads = [
        pltpu.make_async_copy(screened_ref.at[where_ref[3 + n], pl.ds(far_at, panel), :], blocks.at[n], sems.at[n])
        for n in range(2)
    ]
    near = pltpu.make_async_copy(
        screened_ref.at[core, pl.ds(near_at, 2 * panel), :], sent_ref.at[: 2 * panel, :], sems.at[2]
    )
    for c in loads:
        c.start()
    near.start()
    lane = lax.broadcasted_iota(jnp.int32, nodes.shape, 1)
    nu = jnp.full(nodes.shape, nu_ref[core], jnp.float32)
    weight = jnp.full(nodes.shape, weight_ref[core], jnp.float32)
    rest = jnp.where(lane % 2 == 0, nu, weight)
    packed = jnp.zeros(nodes.shape, jnp.float32)
    for n in range(3):
        term = rest.astype(jnp.bfloat16).astype(jnp.float32)
        packed = jnp.where(lane // 2 == n, term, packed)
        rest = rest - term
    nodes[...] = packed.astype(jnp.bfloat16)
    stores = [
        pltpu.make_async_copy(far_ref.at[0], sent_ref.at[2 * panel : 3 * panel, :], sems.at[3]),
        pltpu.make_async_copy(nodes, sent_ref.at[3 * panel :, :], sems.at[4]),
    ]
    stores[1].start()
    for n in range(2):
        loads[n].wait()

        @pl.when(where_ref[0] == 1)
        def _():
            far_ref[n] = blocks[n]

        @pl.when(where_ref[0] == 0)
        def _():
            far_ref[n] = blocks[n].T

        if n == 0:
            stores[0].start()
    for c in stores + [near]:
        c.wait()


def transpose_kernel(block_ref, out_ref):
    out_ref[...] = block_ref[...].T


def run_kernel(kind, plan, where, k_part, mats, arrays, m_dev, begin=0):
    n_rows, panel = mats[0].shape
    n_slots, depth = k_part.shape[0], 2 * panel
    scratch = [
        pltpu.VMEM((n_rows, depth), jnp.bfloat16),
        pltpu.VMEM((n_rows, panel), jnp.bfloat16),
        pltpu.VMEM((n_slots, depth, panel), jnp.bfloat16),
        pltpu.VMEM(k_part.shape, jnp.float32),
        pltpu.SemaphoreType.DMA((6,)),
        pltpu.SemaphoreType.DMA((n_slots,)),
    ]
    flops = 2 * n_rows * depth * panel * n_slots // (16 if kind == "near" else 1)
    return pl.pallas_call(
        functools.partial(quadratic_kernel, plan, m_dev, begin, min(n_rows, 4 * m_dev), kind),
        out_shape=jax.ShapeDtypeStruct((n_rows // m_dev, 8, NW), jnp.float32),
        in_specs=[pl.BlockSpec(memory_space=pltpu.SMEM)]
        + [pl.BlockSpec(memory_space=pl.ANY)] * (1 + len(mats) + len(arrays)),
        out_specs=pl.BlockSpec(memory_space=pltpu.VMEM),
        scratch_shapes=scratch,
        cost_estimate=pl.CostEstimate(flops=flops, bytes_accessed=depth * panel, transcendentals=0),
        compiler_params=pltpu.CompilerParams(vmem_limit_bytes=48 * 2**20),
    )(where, k_part, *mats, *arrays)


def after(value, *others):
    return lax.optimization_barrier((value,) + others)[0]


def square_line(pair_matrix, screened, imag_freq, quad_weight, band_energy, band_index):
    n_dev, m_dev, panel = pair_matrix.shape
    ga = lax.axis_index("ga")
    core = lax.axis_index("band")
    rows = n_dev * m_dev
    own = pair_matrix.reshape(rows, panel)
    end = (ga == 0) | (ga == 3)
    low = ga < 2
    near_at = jnp.where(ga == 0, 0, jnp.where(ga == 3, 2, 1)) * panel
    far_at = (ga + 2) % 4 * panel
    give_at = jnp.where(ga % 2 == 0, 3, 0) * panel
    where = jnp.stack([end, low, near_at, core, 1 - core, far_at]).astype(jnp.int32)

    outer = [(0, 1), (1, 0), (2, 3), (3, 2)]
    inner = [(1, 2), (2, 1)]
    outward = [(1, 0), (2, 3)]

    def piece(start, count):
        return lax.dynamic_slice(screened, (core, start, 0), (1, count, panel))[0]

    def share(block):
        return flip(block, "band", 1)

    given = lax.ppermute(piece(give_at, panel), "ga", outer)
    def local(body, shape, *inputs):
        specs = [pl.BlockSpec(memory_space=pltpu.SMEM if x.dtype == jnp.int32 else pltpu.VMEM) for x in inputs]
        return pl.pallas_call(
            body,
            out_shape=jax.ShapeDtypeStruct(shape, jnp.bfloat16),
            in_specs=specs,
            out_specs=pl.BlockSpec(memory_space=pltpu.VMEM),
            cost_estimate=pl.CostEstimate(flops=0, bytes_accessed=4 * panel * panel, transcendentals=0),
        )(*inputs)

    sent, far_self = pl.pallas_call(
        pack_kernel,
        out_shape=(
            jax.ShapeDtypeStruct((3 * panel + 16, panel), jnp.bfloat16),
            jax.ShapeDtypeStruct((2, panel, panel), jnp.bfloat16),
        ),
        in_specs=[pl.BlockSpec(memory_space=pltpu.SMEM)] * 3 + [pl.BlockSpec(memory_space=pl.ANY)],
        out_specs=(pl.BlockSpec(memory_space=pl.ANY), pl.BlockSpec(memory_space=pltpu.VMEM)),
        scratch_shapes=[
            pltpu.VMEM((2, panel, panel), jnp.bfloat16),
            pltpu.VMEM((16, panel), jnp.bfloat16),
            pltpu.SemaphoreType.DMA((5,)),
        ],
        cost_estimate=pl.CostEstimate(flops=0, bytes_accessed=8 * panel * panel, transcendentals=0),
        compiler_params=pltpu.CompilerParams(vmem_limit_bytes=32 * 2**20),
    )(where, imag_freq, quad_weight, screened)
    cut = 3 * panel // 2
    x1 = flip(sent, "freq", 1)
    y1 = flip(sent, "freq", 2)
    b_rows = lax.ppermute(own, "ga", inner)
    a_rows = lax.ppermute(after(own, given), "ga", outer)
    turned = local(transpose_kernel, (panel, panel), given)
    given_all = lax.all_gather(after(turned, x1, y1, a_rows, b_rows), ("freq", "band"))
    d1a = flip(y1[:cut], "freq", 1)
    d1b = flip(x1[cut:], "freq", 2)
    energies = lookup(band_index, band_energy)
    offsets = make_grid(NW)[None, :] - energies[:, None]
    mine = jnp.stack([imag_freq, quad_weight], axis=1)
    mine = jnp.where(core == 0, mine, mine[::-1])

    def weigh(nodes):
        nu, weight = nodes[:, 0, None, None], nodes[:, 1, None, None]
        return (-weight / math.pi) * (offsets / (offsets * offsets + nu * nu))

    def carried(*places):
        terms = jnp.stack([w[row, :6] for w, row in places]).astype(jnp.float32).reshape(-1, 3, 2)
        return (terms[:, 0] + terms[:, 1]) + terms[:, 2]

    whole = 2 * panel
    panels = (own, a_rows, b_rows)
    slots = [[(0, ("at", 3 + s), ("at", 2), whole)] for s in range(2)]
    slots += [[(r, None, 0, whole)] for r in (1, 2)]
    k_here = weigh(jnp.concatenate([mine, carried((x1, 3 * panel), (y1, 3 * panel))]))
    near = run_kernel("near", slots, where, k_here, panels, (screened, x1, y1), m_dev)

    c_rows = lax.ppermute(b_rows, "ga", outward)
    d_rows = lax.ppermute(a_rows, "ga", inner)
    x1_o, y1_o = share(after(x1, d1a, d1b, near)), share(after(y1, d1a, d1b, near))
    d1a_o, d1b_o = share(after(d1a, c_rows, d_rows)), share(after(d1b, c_rows, d_rows))
    slots = [[(r, None, 0, whole)] for r in (0, 1)]
    slots += [[(r, None, 0, cut), (r + 1, None, 0, whole - cut)] for r in (2, 4)]
    k_there = weigh(carried((x1_o, 3 * panel), (y1_o, 3 * panel), (d1b, cut), (d1b_o, cut)))
    corner = run_kernel("near", slots, where, k_there, panels, (x1_o, y1_o, d1a, d1b, d1a_o, d1b_o), m_dev)
    k_all = jnp.concatenate([k_here, k_there])

    square = lax.axis_index("freq")
    order = ((0, core), (0, 1 - core), (1, core), (2, core), (1, 1 - core), (2, 1 - core), (3, core), (3, 1 - core))
    ranks = jnp.stack([(square ^ r) * 2 + c for r, c in order]).astype(jnp.int32)
    sources = [(1, 0, 0), (1, 1, 0)] + [(r, None, whole) for r in (2, 3, 4, 5)] + [(r, None, whole - cut) for r in (6, 7)]
    slots = [[(*src, panel), (0, ("at", 6 + n), 0, panel)] for n, src in enumerate(sources)]
    arrays = (given_all, far_self, x1, y1, x1_o, y1_o, d1b, d1b_o)
    far = run_kernel(
        "far", slots, jnp.concatenate([where, ranks]), k_all,
        (own, a_rows, b_rows), (c_rows, d_rows, *arrays), m_dev,
    )
    sigma = jnp.sum(near + corner + far, axis=1)
    for axis in ("freq", "ga"):
        t1, t2, t3 = (flip(sigma, axis, r) for r in (1, 2, 3))
        sigma = (sigma + t1) + (t2 + t3)
    return sigma


def on_device(pair_matrix, screened, *rest):
    sizes = tuple(lax.axis_size(a) for a in ("freq", "ga", "band"))
    fits = sizes == (4, 4, 2) and screened.shape[0] == 2 and pair_matrix.shape[0] % 8 == 0
    return (square_line if fits else general)(pair_matrix, screened, *rest)


def solution(mesh):
    placed = (P("band", "freq", "ga"), P("freq", None, "ga"), P("freq"), P("freq"), P(), P("freq"))
    return jax.shard_map(
        on_device, mesh=mesh, in_specs=placed, out_specs=P("band", None), check_vma=False
    )
```

```python
import functools
import math

import jax
import jax.numpy as jnp
from jax import lax
from jax.experimental import pallas as pl
from jax.experimental.pallas import tpu as pltpu
from jax.sharding import PartitionSpec as P

NW = 256

omega_low = -10.0
omega_span = 20.0


def make_grid(count):
    return omega_low + omega_span * jnp.arange(count, dtype=jnp.float32) / (count - 1)


def lookup(indices, table):
    hit = indices[:, None] == jnp.arange(table.shape[0], dtype=jnp.int32)[None, :]
    return jnp.sum(jnp.where(hit, table[None, :], 0.0), axis=1)


def from_behind(block, axis, distance):
    devices = range(lax.axis_size(axis))
    route = [((i - distance) % len(devices), i) for i in devices]
    return lax.ppermute(block, axis, route)


def flip(block, axis, bits):
    return lax.ppermute(block, axis, [(i, i ^ bits) for i in range(lax.axis_size(axis))])


def contribute(full_rows, panel_rows, w_mat, nu_val, weight_val, energies, omega_grid, n_dev):
    product = jnp.dot(full_rows, w_mat, preferred_element_type=jnp.float32)
    contract = jnp.sum(product * panel_rows.astype(jnp.float32), axis=-1).reshape(n_dev, -1)
    offsets = omega_grid[None, :] - energies[:, None]
    kernel = offsets / (offsets * offsets + nu_val * nu_val)
    return -weight_val / math.pi * jnp.dot(contract, kernel, precision=lax.Precision.HIGHEST)


def general(pair_matrix, screened, imag_freq, quad_weight, band_energy, band_index):
    n_dev, m_dev, g_panel = pair_matrix.shape
    f_dev = screened.shape[0]
    cycle_size = lax.axis_size("freq")
    cycle_pos = lax.axis_index("freq")
    full_pairs = lax.all_gather(pair_matrix, "ga", axis=2, tiled=True)
    g_all = full_pairs.shape[2]
    omega_grid = make_grid(NW)
    sigma_part = jnp.zeros((n_dev, NW), jnp.float32)
    panel_rows = pair_matrix.reshape(n_dev * m_dev, g_panel)
    full_rows = full_pairs.reshape(n_dev * m_dev, g_all)
    energies = lookup(band_index, band_energy)
    nu_all = lax.all_gather(imag_freq, "freq", axis=0, tiled=True)
    weight_all = lax.all_gather(quad_weight, "freq", axis=0, tiled=True)
    w_slab = screened
    for turn_index in range(cycle_size):
        source = jnp.mod(cycle_pos - turn_index, cycle_size)
        nu_vals = lax.dynamic_slice_in_dim(nu_all, source * f_dev, f_dev)
        weight_vals = lax.dynamic_slice_in_dim(weight_all, source * f_dev, f_dev)
        for slot in range(f_dev):
            sigma_part = sigma_part + contribute(
                full_rows, panel_rows, w_slab[slot], nu_vals[slot], weight_vals[slot],
                energies, omega_grid, n_dev,
            )
        if turn_index + 1 < cycle_size:
            w_slab = from_behind(w_slab, "freq", 1)
    return lax.psum(sigma_part, ("freq", "ga"))


def choose(flag, yes, no):
    @pl.when(flag == 1)
    def _():
        yes.start()

    @pl.when(flag == 0)
    def _():
        no.start()


def start_slot(plan, slot, where_ref, refs, w_all, w_sems):
    at = 0
    for index, lead, begin, count in plan[slot]:
        src = refs[index]
        if lead is not None:
            src = src.at[where_ref[lead[1]] if isinstance(lead, tuple) else lead]
        if isinstance(begin, tuple):
            begin = pl.multiple_of(where_ref[begin[1]], count // 2)
        src = src.at[pl.ds(begin, count), :]
        pltpu.make_async_copy(src, w_all.at[slot, at : at + count, :], w_sems.at[slot]).start()
        at += count


def quadratic_kernel(plan, m_dev, skip, tile, kind, where_ref, k_ref, own_ref, a_ref, b_ref, *rest):
    refs = rest[: len(rest) - 7]
    out_ref, left, right, w_all, k_all, sems, w_sems = rest[len(rest) - 7 :]
    n_slots, _, panel = w_all.shape
    end, low = where_ref[0], where_ref[1]
    if kind == "near":
        w_refs = refs
        here = left.at[:, pl.ds(pl.multiple_of((1 - low) * panel, panel), panel)]
        there = left.at[:, pl.ds(pl.multiple_of(low * panel, panel), panel)]
        fixed = [(own_ref, here), (own_ref, right)]
        either = [((a_ref, b_ref), there)]
    else:
        c_ref, d_ref, w_refs = refs[0], refs[1], refs[2:]
        fixed = [(a_ref, left.at[:, panel:])]
        either = [((c_ref, own_ref), left.at[:, :panel]), ((own_ref, d_ref), right)]
    start_slot(plan, 0, where_ref, w_refs, w_all, w_sems)
    waits = [pltpu.make_async_copy(src, dst, sems.at[n]) for n, (src, dst) in enumerate(fixed)]
    for c in waits:
        c.start()
    for n, ((yes, no), dst) in enumerate(either):
        sem = sems.at[len(fixed) + n]
        waits.append(pltpu.make_async_copy(yes, dst, sem))
        choose(end, waits[-1], pltpu.make_async_copy(no, dst, sem))
    waits.append(pltpu.make_async_copy(k_ref.at[skip : skip + n_slots], k_all, sems.at[5]))
    waits[-1].start()
    for slot in range(1, n_slots):
        start_slot(plan, slot, where_ref, w_refs, w_all, w_sems)
    out_ref[...] = jnp.zeros_like(out_ref)
    for c in waits:
        c.wait()

    def one(slot, carry):
        pltpu.make_async_copy(w_all.at[slot], w_all.at[slot], w_sems.at[slot]).wait()
        for t in range(right.shape[0] // tile):
            at = slice(t * tile, (t + 1) * tile)
            y = jnp.dot(left[at], w_all[slot], preferred_element_type=jnp.float32)
            c = jnp.sum(y * right[at].astype(jnp.float32), axis=1, keepdims=True)
            for k in range(tile // m_dev):
                term = c[k * m_dev : (k + 1) * m_dev] * k_all[slot]
                out_ref[t * (tile // m_dev) + k] += jnp.sum(term.reshape(m_dev // 8, 8, NW), axis=0)
        return carry

    lax.fori_loop(0, n_slots, one, 0)


def pack_kernel(where_ref, nu_ref, weight_ref, screened_ref, sent_ref, far_ref, blocks, nodes, sems):
    panel = blocks.shape[1]
    core = where_ref[3]
    near_at = pl.multiple_of(where_ref[2], panel)
    far_at = pl.multiple_of(where_ref[5], panel)
    loads = [
        pltpu.make_async_copy(screened_ref.at[where_ref[3 + n], pl.ds(far_at, panel), :], blocks.at[n], sems.at[n])
        for n in range(2)
    ]
    near = pltpu.make_async_copy(
        screened_ref.at[core, pl.ds(near_at, 2 * panel), :], sent_ref.at[: 2 * panel, :], sems.at[2]
    )
    for c in loads:
        c.start()
    near.start()
    lane = lax.broadcasted_iota(jnp.int32, nodes.shape, 1)
    nu = jnp.full(nodes.shape, nu_ref[core], jnp.float32)
    weight = jnp.full(nodes.shape, weight_ref[core], jnp.float32)
    rest = jnp.where(lane % 2 == 0, nu, weight)
    packed = jnp.zeros(nodes.shape, jnp.float32)
    for n in range(3):
        term = rest.astype(jnp.bfloat16).astype(jnp.float32)
        packed = jnp.where(lane // 2 == n, term, packed)
        rest = rest - term
    nodes[...] = packed.astype(jnp.bfloat16)
    stores = [
        pltpu.make_async_copy(far_ref.at[0], sent_ref.at[2 * panel : 3 * panel, :], sems.at[3]),
        pltpu.make_async_copy(nodes, sent_ref.at[3 * panel :, :], sems.at[4]),
    ]
    stores[1].start()
    for n in range(2):
        loads[n].wait()

        @pl.when(where_ref[0] == 1)
        def _():
            far_ref[n] = blocks[n]

        @pl.when(where_ref[0] == 0)
        def _():
            far_ref[n] = blocks[n].T

        if n == 0:
            stores[0].start()
    for c in stores + [near]:
        c.wait()


def transpose_kernel(block_ref, out_ref):
    out_ref[...] = block_ref[...].T


def run_kernel(kind, plan, where, k_part, mats, arrays, m_dev, skip=0):
    n_rows, panel = mats[0].shape
    n_slots, depth = len(plan), 2 * panel
    scratch = [
        pltpu.VMEM((n_rows, depth), jnp.bfloat16),
        pltpu.VMEM((n_rows, panel), jnp.bfloat16),
        pltpu.VMEM((n_slots, depth, panel), jnp.bfloat16),
        pltpu.VMEM((n_slots, *k_part.shape[1:]), jnp.float32),
        pltpu.SemaphoreType.DMA((6,)),
        pltpu.SemaphoreType.DMA((n_slots,)),
    ]
    flops = 2 * n_rows * depth * panel * n_slots // (16 if kind == "near" else 1)
    return pl.pallas_call(
        functools.partial(quadratic_kernel, plan, m_dev, skip, min(n_rows, 4 * m_dev), kind),
        out_shape=jax.ShapeDtypeStruct((n_rows // m_dev, 8, NW), jnp.float32),
        in_specs=[pl.BlockSpec(memory_space=pltpu.SMEM)]
        + [pl.BlockSpec(memory_space=pl.ANY)] * (1 + len(mats) + len(arrays)),
        out_specs=pl.BlockSpec(memory_space=pltpu.VMEM),
        scratch_shapes=scratch,
        cost_estimate=pl.CostEstimate(flops=flops, bytes_accessed=depth * panel, transcendentals=0),
        compiler_params=pltpu.CompilerParams(vmem_limit_bytes=48 * 2**20),
    )(where, k_part, *mats, *arrays)


def after(value, *others):
    return lax.optimization_barrier((value,) + others)[0]


def square_line(pair_matrix, screened, imag_freq, quad_weight, band_energy, band_index):
    n_dev, m_dev, panel = pair_matrix.shape
    ga = lax.axis_index("ga")
    core = lax.axis_index("band")
    rows = n_dev * m_dev
    own = pair_matrix.reshape(rows, panel)
    end = (ga == 0) | (ga == 3)
    low = ga < 2
    near_at = jnp.where(ga == 0, 0, jnp.where(ga == 3, 2, 1)) * panel
    far_at = (ga + 2) % 4 * panel
    give_at = jnp.where(ga % 2 == 0, 3, 0) * panel
    where = jnp.stack([end, low, near_at, core, 1 - core, far_at]).astype(jnp.int32)

    outer = [(0, 1), (1, 0), (2, 3), (3, 2)]
    inner = [(1, 2), (2, 1)]
    outward = [(1, 0), (2, 3)]

    def piece(start, count):
        return lax.dynamic_slice(screened, (core, start, 0), (1, count, panel))[0]

    def share(block):
        return flip(block, "band", 1)

    given = lax.ppermute(piece(give_at, panel), "ga", outer)
    def local(body, shape, *inputs):
        specs = [pl.BlockSpec(memory_space=pltpu.SMEM if x.dtype == jnp.int32 else pltpu.VMEM) for x in inputs]
        return pl.pallas_call(
            body,
            out_shape=jax.ShapeDtypeStruct(shape, jnp.bfloat16),
            in_specs=specs,
            out_specs=pl.BlockSpec(memory_space=pltpu.VMEM),
            cost_estimate=pl.CostEstimate(flops=0, bytes_accessed=4 * panel * panel, transcendentals=0),
        )(*inputs)

    sent, far_self = pl.pallas_call(
        pack_kernel,
        out_shape=(
            jax.ShapeDtypeStruct((3 * panel + 16, panel), jnp.bfloat16),
            jax.ShapeDtypeStruct((2, panel, panel), jnp.bfloat16),
        ),
        in_specs=[pl.BlockSpec(memory_space=pltpu.SMEM)] * 3 + [pl.BlockSpec(memory_space=pl.ANY)],
        out_specs=(pl.BlockSpec(memory_space=pl.ANY), pl.BlockSpec(memory_space=pltpu.VMEM)),
        scratch_shapes=[
            pltpu.VMEM((2, panel, panel), jnp.bfloat16),
            pltpu.VMEM((16, panel), jnp.bfloat16),
            pltpu.SemaphoreType.DMA((5,)),
        ],
        cost_estimate=pl.CostEstimate(flops=0, bytes_accessed=8 * panel * panel, transcendentals=0),
        compiler_params=pltpu.CompilerParams(vmem_limit_bytes=32 * 2**20),
    )(where, imag_freq, quad_weight, screened)
    cut = 3 * panel // 2
    x1 = flip(sent, "freq", 1)
    y1 = flip(sent, "freq", 2)
    b_rows = lax.ppermute(own, "ga", inner)
    a_rows = lax.ppermute(after(own, given), "ga", outer)
    turned = local(transpose_kernel, (panel, panel), given)
    given_all = lax.all_gather(after(turned, x1, y1, a_rows, b_rows), ("freq", "band"))
    d1a = flip(y1[:cut], "freq", 1)
    d1b = flip(x1[cut:], "freq", 2)
    energies = lookup(band_index, band_energy)
    offsets = make_grid(NW)[None, :] - energies[:, None]
    mine = jnp.stack([imag_freq, quad_weight], axis=1)
    mine = jnp.where(core == 0, mine, mine[::-1])

    def weigh(nodes):
        nu, weight = nodes[:, 0, None, None], nodes[:, 1, None, None]
        return (-weight / math.pi) * (offsets / (offsets * offsets + nu * nu))

    def carried(*places):
        terms = jnp.stack([w[row, :6] for w, row in places]).astype(jnp.float32).reshape(-1, 3, 2)
        return (terms[:, 0] + terms[:, 1]) + terms[:, 2]

    whole = 2 * panel
    panels = (own, a_rows, b_rows)
    slots = [[(0, ("at", 3 + s), ("at", 2), whole)] for s in range(2)]
    slots += [[(r, None, 0, whole)] for r in (1, 2)]
    here = jnp.concatenate([mine, carried((x1, 3 * panel), (y1, 3 * panel))])
    k_here = weigh(here)
    near = run_kernel("near", slots, where, k_here, panels, (screened, x1, y1), m_dev)

    c_rows = lax.ppermute(b_rows, "ga", outward)
    d_rows = lax.ppermute(a_rows, "ga", inner)
    x1_o, y1_o = share(after(x1, d1a, d1b, near)), share(after(y1, d1a, d1b, near))
    d1a_o, d1b_o = share(after(d1a, c_rows, d_rows)), share(after(d1b, c_rows, d_rows))
    slots = [[(r, None, 0, whole)] for r in (0, 1)]
    slots += [[(r, None, 0, cut), (r + 1, None, 0, whole - cut)] for r in (2, 4)]
    there = carried((x1_o, 3 * panel), (y1_o, 3 * panel), (d1b, cut), (d1b_o, cut))
    k_all = weigh(jnp.concatenate([here, there]))
    corner = run_kernel("near", slots, where, k_all, panels, (x1_o, y1_o, d1a, d1b, d1a_o, d1b_o), m_dev, 4)

    square = lax.axis_index("freq")
    order = ((0, core), (0, 1 - core), (1, core), (2, core), (1, 1 - core), (2, 1 - core), (3, core), (3, 1 - core))
    ranks = jnp.stack([(square ^ r) * 2 + c for r, c in order]).astype(jnp.int32)
    sources = [(1, 0, 0), (1, 1, 0)] + [(r, None, whole) for r in (2, 3, 4, 5)] + [(r, None, whole - cut) for r in (6, 7)]
    slots = [[(*src, panel), (0, ("at", 6 + n), 0, panel)] for n, src in enumerate(sources)]
    arrays = (given_all, far_self, x1, y1, x1_o, y1_o, d1b, d1b_o)
    far = run_kernel(
        "far", slots, jnp.concatenate([where, ranks]), k_all,
        (own, a_rows, b_rows), (c_rows, d_rows, *arrays), m_dev,
    )
    sigma = jnp.sum(near + corner + far, axis=1)
    for axis in ("freq", "ga"):
        t1, t2, t3 = (flip(sigma, axis, r) for r in (1, 2, 3))
        sigma = (sigma + t1) + (t2 + t3)
    return sigma


def on_device(pair_matrix, screened, *rest):
    sizes = tuple(lax.axis_size(a) for a in ("freq", "ga", "band"))
    fits = sizes == (4, 4, 2) and screened.shape[0] == 2 and pair_matrix.shape[0] % 8 == 0
    return (square_line if fits else general)(pair_matrix, screened, *rest)


def solution(mesh):
    placed = (P("band", "freq", "ga"), P("freq", None, "ga"), P("freq"), P("freq"), P(), P("freq"))
    return jax.shard_map(
        on_device, mesh=mesh, in_specs=placed, out_specs=P("band", None), check_vma=False
    )
```
